512 devices in a mesh: dp: 64 (over z_lo, x, y), tensor: 8 (over z_hi, core).
Axes of the slice: x: 4, y: 8, z: 8 (z_hi: 4, z_lo: 2; z = z_hi * 2 + z_lo), core: 2. Of those that a mesh axis runs over, the one named last changes fastest.
Arguments:
- image_embedding_matrix: float32 [1152, 32768], P('tensor', 'dp'), may hold values from -0.1875 to 0.1875
- words_embedding_matrix: float32 [1152, 32768], P('tensor', 'dp'), may hold values from -0.1875 to 0.1875
- natural_exponent_heat: float32 [1], replicated, may hold values from 2 to 2.5
- offset_term_array: float32 [1], replicated, may hold values from -2 to -1
Outputs:
- image_grad: float32 [1152, 32768], P('tensor', 'dp')
- text_grad: float32 [1152, 32768], P('tensor', 'dp')
The draws below stay inside these ranges and needn't reach their ends.
All inputs are finite; a program needn't handle non-finite values.
Results may differ from the reference program's by a relative error of at most 0.0001.
Values sent between devices are 32-bit elements; how exact they have to be, the bound alone decides.
A program may use at most 64 MiB of HBM per device.

```python
import jax
import jax.numpy as jnp
from jax import lax

D = 1152
ROWS = 512
SHIFTS = 4
TOKENS = 32768
N_DP = 64


def block_scale(own_key, extent, cuts, low, top_value):
    def one(axis_at, shards_of):
        heights = jax.random.uniform(jax.random.fold_in(jax.random.fold_in(own_key, 6), axis_at), (shards_of,), jnp.float32, low / len(cuts), top_value / len(cuts))
        return jnp.repeat(jnp.exp(heights), extent[axis_at] // shards_of).reshape((-1,) + (1,) * (len(extent) - axis_at - 1))

    factor_of = one(*cuts[0])
    for cut in cuts[1:]:
        factor_of = factor_of * one(*cut)
    return factor_of


def gaussian(rng, shape, spread, bound, pieces=(), kind=jnp.bfloat16):
    array = jax.random.normal(rng, shape, jnp.float32) * spread
    if len(pieces) > 0:
        array = block_scale(rng, shape, pieces, -0.22, 0.18) * array
    return jnp.clip(array, min=-bound, max=bound).astype(kind)


def setup_inputs(seed: int = 0) -> dict:
    key_of = jax.random.split(jax.random.key(seed), 5)
    return {
        "image_embedding_matrix": gaussian(key_of[0], (D, TOKENS), D ** -0.5, 0.1875, ((0, 8), (1, 64)), jnp.float32),
        "words_embedding_matrix": gaussian(key_of[1], (D, TOKENS), D ** -0.5, 0.1875, ((0, 8), (1, 64)), jnp.float32),
        "natural_exponent_heat": jnp.clip(jax.random.uniform(key_of[2], (1,), jnp.float32, 2.0, 2.5), 2.0, 2.5),
        "offset_term_array": jnp.clip(jax.random.uniform(key_of[3], (1,), jnp.float32, -2.0, -1.0), -2.0, -1.0),
    }


def reference(image_embedding_matrix, words_embedding_matrix, natural_exponent_heat, offset_term_array):
    heat_factor = jnp.exp(natural_exponent_heat[0])
    segment_offset_amount = offset_term_array[0]
    image_segment_array = image_embedding_matrix.reshape(D, N_DP, ROWS)
    text_blocks = words_embedding_matrix.reshape(D, N_DP, ROWS)
    diagonal_ones = jnp.eye(ROWS, dtype=jnp.float32)
    image_slope_total = jnp.zeros((D, N_DP, ROWS), jnp.float32)
    text_total = jnp.zeros((D, N_DP, ROWS), jnp.float32)
    for shift_counter in range(SHIFTS):
        cycled_segments = jnp.roll(text_blocks, shift_counter, axis=1)
        cosine_product_matrix = jnp.einsum("dnr,dnk->nrk", image_segment_array, cycled_segments, precision=lax.Precision.HIGHEST)
        squashing_slope_factor = jax.nn.sigmoid(heat_factor * cosine_product_matrix + segment_offset_amount)
        if shift_counter == 0:
            squashing_slope_factor = squashing_slope_factor - diagonal_ones
        image_slope_total = image_slope_total + heat_factor * jnp.einsum("jfr,qjr->qjf", squashing_slope_factor, cycled_segments, precision=lax.Precision.HIGHEST)
        words_partial_share = heat_factor * jnp.einsum("jyu,kjy->kju", squashing_slope_factor, image_segment_array, precision=lax.Precision.HIGHEST)
        text_total = text_total + jnp.roll(words_partial_share, -shift_counter, axis=1)
    return image_slope_total.reshape(D, N_DP * ROWS), text_total.reshape(D, N_DP * ROWS)
```

```python
import jax
import jax.numpy as jnp
from jax import lax
from jax.experimental import pallas as pl
from jax.experimental.pallas import tpu as pltpu
from jax.sharding import PartitionSpec as P

SHIFTS = 4
N_Q = 4
MESH = pl.DeviceIdType.MESH
F32 = jnp.float32
BF16 = jnp.bfloat16

A_DIRECT_P, A_DIRECT_M, A_HALF_P, A_HALF_M, A_ON_P, A_ON_M = range(6)
T_SIB, T_OWN_P, T_OWN_M, T_SIB_P, T_SIB_M, T_ON_P, T_ON_M = range(6, 13)
B_FAR_P, B_FAR_M, B_NEAR_P, B_NEAR_M, B_SUM_P, B_SUM_M, B_SIB = range(13, 20)
E_DIRECT_P, E_DIRECT_M, E_HALF_P, E_HALF_M, E_ON_P, E_ON_M = range(20, 26)
G_SIB = 26
I_SIB = 30
CHAIN = 46
BACK = 58
N_SEMS = 70


def split(value):
    high = value.astype(BF16)
    return high, (value - high.astype(F32)).astype(BF16)


def dot3(a_high, a_low, b_high, b_low, dims):
    def one(a, b):
        return lax.dot_general(a, b, (dims, ((), ())), preferred_element_type=F32)

    return one(a_high, b_high) + (one(a_high, b_low) + one(a_low, b_high))


def kernel(
    n_dp,
    heat_ref,
    bias_ref,
    img_ref,
    txt_ref,
    gi_ref,
    gt_ref,
    text,
    image,
    t_high,
    t_low,
    i_high,
    i_low,
    g_text,
    g_image,
    g_other,
    back,
    far_in,
    near_in,
    keep,
    half_in,
    send_sem,
    recv_sem,
):
    d, rows = img_ref.shape
    half, piece = rows // 2, rows // N_Q
    dp, t = lax.axis_index("dp"), lax.axis_index("tensor")
    q, c = t // 2, t % 2
    o = 1 - c
    at = [lax.rem(q + r, N_Q) for r in range(N_Q)]
    sib = (dp, 2 * q + o)
    up, down = (dp, 2 * at[1] + c), (dp, 2 * at[3] + c)
    after, before = (lax.rem(dp + 1, n_dp), t), (lax.rem(dp + n_dp - 1, n_dp), t)
    started = []

    def send(index, src, dst, device):
        copy = pltpu.make_async_remote_copy(
            src_ref=src,
            dst_ref=dst,
            send_sem=send_sem.at[index],
            recv_sem=recv_sem.at[index],
            device_id=device,
            device_id_type=MESH,
        )
        copy.start()
        started.append(copy)

    def arrive(index, dst):
        pltpu.make_async_remote_copy(
            src_ref=dst,
            dst_ref=dst,
            send_sem=send_sem.at[index],
            recv_sem=recv_sem.at[index],
            device_id=sib,
            device_id_type=MESH,
        ).wait_recv()

    def piece_of(ref, r, first=0, count=None):
        cols = pl.ds(pl.multiple_of(at[r] * piece, piece), piece)
        return ref.at[pl.ds(first, d if count is None else count), cols]

    def half_of(ref, which):
        return ref.at[:, pl.ds(pl.multiple_of(which * half, half), half)]

    barrier = pltpu.get_barrier_semaphore()
    partners = (sib, up, down, after, before)
    for partner in partners:
        pl.semaphore_signal(barrier, inc=1, device_id=partner, device_id_type=MESH)
    pl.semaphore_wait(barrier, len(partners))

    h = d // 2
    send(A_HALF_P, piece_of(img_ref, 2, 0, h), half_in.at[0], up)
    send(A_HALF_M, piece_of(img_ref, 2, h, h), half_in.at[1], down)
    image[0, c, q] = piece_of(img_ref, 0)[...]

    def chain(k, r):
        if k < SHIFTS - 1:
            send(CHAIN + 4 * k + r, image.at[k, c, at[r]], image.at[k + 1, c, at[r]], before)
        send(I_SIB + 4 * k + r, image.at[k, c, at[r]], image.at[k, c, at[r]], sib)

    def chained(k, r):
        arrive(CHAIN + 4 * (k - 1) + r, image.at[k, c, at[r]])
        chain(k, r)

    chain(0, 0)
    send(A_DIRECT_P, piece_of(img_ref, 1), image.at[0, c, q], up)
    send(A_DIRECT_M, piece_of(img_ref, 3), image.at[0, c, q], down)
    send(T_SIB, half_of(txt_ref, o), text.at[c, q], sib)
    text[c, q] = half_of(txt_ref, c)[...]

    arrive(A_HALF_P, half_in.at[0])
    send(A_ON_P, half_in.at[0], image.at[0, c, at[3], pl.ds(0, h)], up)
    arrive(A_HALF_M, half_in.at[1])
    send(A_ON_M, half_in.at[1], image.at[0, c, at[1], pl.ds(h, h)], down)
    send(T_OWN_P, text.at[c, q], text.at[c, q], up)
    send(T_OWN_M, text.at[c, q], text.at[c, q], down)

    chained(1, 0)
    arrive(A_DIRECT_P, image.at[0, c, at[3]])
    chain(0, 3)
    arrive(A_DIRECT_M, image.at[0, c, at[1]])
    chain(0, 1)
    arrive(T_SIB, text.at[o, q])
    send(T_SIB_P, text.at[o, q], text.at[o, q], up)
    send(T_SIB_M, text.at[o, q], text.at[o, q], down)
    arrive(A_ON_P, image.at[0, c, at[2], pl.ds(0, h)])
    arrive(A_ON_M, image.at[0, c, at[2], pl.ds(h, h)])
    chain(0, 2)
    chained(2, 0)
    chained(1, 3)
    chained(1, 1)
    arrive(T_OWN_P, text.at[c, at[3]])
    send(T_ON_P, text.at[c, at[3]], text.at[c, at[3]], up)
    chained(1, 2)
    chained(3, 0)
    chained(2, 3)
    chained(2, 1)
    arrive(T_OWN_M, text.at[c, at[1]])
    arrive(T_SIB_M, text.at[o, at[1]])
    send(T_ON_M, text.at[o, at[1]], text.at[o, at[1]], down)
    chained(2, 2)

    def text_ready(part, r):
        t_high[part, at[r]], t_low[part, at[r]] = split(text[part, at[r]])

    def image_ready(k, part, r):
        cols = slice(k * piece, (k + 1) * piece)
        i_high[part, at[r], :, cols], i_low[part, at[r], :, cols] = split(image[k, part, at[r]])

    def image_sibling(k, r):
        arrive(I_SIB + 4 * k + r, image.at[k, o, at[r]])
        image_ready(k, o, r)

    text_ready(c, 0)
    text_ready(o, 0)
    text_ready(c, 3)
    text_ready(c, 1)
    text_ready(o, 1)
    for k in range(SHIFTS - 1):
        for r in (0, 3, 1, 2):
            image_ready(k, c, r)
            image_sibling(k, r)
    for r in (3, 1, 2):
        chained(3, r)
    for r in (0, 3, 1, 2):
        image_ready(3, c, r)
        image_sibling(3, r)
    arrive(T_SIB_P, text.at[o, at[3]])
    text_ready(o, 3)
    arrive(T_ON_P, text.at[c, at[2]])
    text_ready(c, 2)
    arrive(T_ON_M, text.at[o, at[2]])
    text_ready(o, 2)

    depth = 2 * N_Q * d
    th, tl = t_high[...].reshape(depth, half), t_low[...].reshape(depth, half)
    ih, il = i_high[...].reshape(depth, rows), i_low[...].reshape(depth, rows)
    dots = dot3(th, tl, ih, il, ((0,), (0,)))
    heat = jnp.exp(jnp.full((1, rows), heat_ref[0], F32))
    slope = jax.nn.sigmoid(heat * dots + bias_ref[0])
    text_id = lax.broadcasted_iota(jnp.int32, slope.shape, 0) + c * half
    image_id = lax.broadcasted_iota(jnp.int32, slope.shape, 1)
    match = (image_id < piece) & (text_id == image_id + q * piece)
    slope = heat * (slope - jnp.where(match, 1.0, 0.0).astype(F32))
    sh, sl = split(slope)

    def image_gradient(ks):
        lo, hi = ks[0] * piece, (ks[-1] + 1) * piece
        grad = dot3(th, tl, sh[:, lo:hi], sl[:, lo:hi], ((1,), (0,)))
        grad = grad.reshape(2, N_Q, d, hi - lo)
        for i, k in enumerate(ks):
            g_image[k] = grad[..., i * piece : (i + 1) * piece]
            send(G_SIB + k, g_image.at[k, o], g_other.at[k], sib)

    def text_gradient(r):
        for part in range(2):
            g_text[part, at[r]] = dot3(
                i_high[part, at[r]], i_low[part, at[r]], sh, sl, ((1,), (1,))
            )

    def add_sibling(k):
        arrive(G_SIB + k, g_other.at[k])
        g_image[k, c] += g_other[k]

    def returned(step, r):
        slot = back.at[step, at[r]]
        arrive(BACK + 4 * step + r, slot)
        slot[...] += g_image[2 - step, c, at[r]]

    order = (2, 1, 3, 0)
    image_gradient((2, 3))
    text_gradient(2)
    send(B_FAR_P, g_text.at[0, at[2]], far_in.at[0], up)
    send(B_FAR_M, g_text.at[1, at[2]], far_in.at[1], down)
    add_sibling(3)
    for r in order:
        send(BACK + r, g_image.at[3, c, at[r]], back.at[0, at[r]], after)
    text_gradient(1)
    send(B_NEAR_P, g_text.at[1, at[1]], near_in.at[0], up)
    text_gradient(3)
    send(B_NEAR_M, g_text.at[0, at[3]], near_in.at[1], down)
    image_gradient((0, 1))
    add_sibling(2)
    text_gradient(0)
    for r in order:
        returned(0, r)
        send(BACK + 4 + r, back.at[0, at[r]], back.at[1, at[r]], after)
    add_sibling(1)
    add_sibling(0)
    arrive(B_FAR_P, far_in.at[0])
    g_text[0, at[1]] += far_in[0]
    send(B_SUM_P, g_text.at[0, at[1]], near_in.at[2], up)
    arrive(B_FAR_M, far_in.at[1])
    g_text[1, at[3]] += far_in[1]
    send(B_SUM_M, g_text.at[1, at[3]], near_in.at[3], down)
    for r in order:
        returned(1, r)
        send(BACK + 8 + r, back.at[1, at[r]], back.at[2, at[r]], after)

    arrive(B_NEAR_P, near_in.at[0])
    arrive(B_NEAR_M, near_in.at[1])
    arrive(B_SUM_P, near_in.at[2])
    arrive(B_SUM_M, near_in.at[3])
    g_text[0, q] += near_in[1] + near_in[2]
    g_text[1, q] += near_in[0] + near_in[3]
    keep[...] = g_text[o, q]
    send(B_SIB, keep, half_of(gt_ref, c), sib)
    half_of(gt_ref, c)[...] = g_text[c, q]

    def own_columns(r, first=0, count=None):
        return piece_of(gi_ref, r, first, count)

    returned(2, 2)
    send(E_HALF_P, back.at[2, at[2], pl.ds(0, h)], half_in.at[2], up)
    send(E_HALF_M, back.at[2, at[2], pl.ds(h, h)], half_in.at[3], down)
    returned(2, 1)
    send(E_DIRECT_P, back.at[2, at[1]], own_columns(0), up)
    returned(2, 3)
    send(E_DIRECT_M, back.at[2, at[3]], own_columns(0), down)
    arrive(E_HALF_P, half_in.at[2])
    send(E_ON_P, half_in.at[2], own_columns(3, 0, h), up)
    arrive(E_HALF_M, half_in.at[3])
    send(E_ON_M, half_in.at[3], own_columns(1, h, h), down)
    returned(2, 0)
    own_columns(0)[...] = back[2, q]
    arrive(E_DIRECT_P, own_columns(3))
    arrive(E_DIRECT_M, own_columns(1))
    arrive(E_ON_P, own_columns(2, 0, h))
    arrive(E_ON_M, own_columns(2, h, h))
    arrive(B_SIB, half_of(gt_ref, o))
    for copy in started:
        copy.wait_send()


def shards(image_shard, text_shard, heat, bias):
    d, rows = image_shard.shape
    half, piece = rows // 2, rows // N_Q
    vmem = pl.BlockSpec(memory_space=pltpu.VMEM)
    smem = pl.BlockSpec(memory_space=pltpu.SMEM)
    n_dp = lax.axis_size("dp")

    def body(*refs):
        kernel(n_dp, *refs)

    return pl.pallas_call(
        body,
        out_shape=(jax.ShapeDtypeStruct((d, rows), F32), jax.ShapeDtypeStruct((d, rows), F32)),
        in_specs=[smem, smem, vmem, vmem],
        out_specs=(vmem, vmem),
        scratch_shapes=[
            pltpu.VMEM((2, N_Q, d, half), F32),
            pltpu.VMEM((SHIFTS, 2, N_Q, d, piece), F32),
            pltpu.VMEM((2, N_Q, d, half), BF16),
            pltpu.VMEM((2, N_Q, d, half), BF16),
            pltpu.VMEM((2, N_Q, d, rows), BF16),
            pltpu.VMEM((2, N_Q, d, rows), BF16),
            pltpu.VMEM((2, N_Q, d, half), F32),
            pltpu.VMEM((SHIFTS, 2, N_Q, d, piece), F32),
            pltpu.VMEM((SHIFTS, N_Q, d, piece), F32),
            pltpu.VMEM((SHIFTS - 1, N_Q, d, piece), F32),
            pltpu.VMEM((2, d, half), F32),
            pltpu.VMEM((4, d, half), F32),
            pltpu.VMEM((d, half), F32),
            pltpu.VMEM((4, d // 2, piece), F32),
            pltpu.SemaphoreType.DMA((N_SEMS,)),
            pltpu.SemaphoreType.DMA((N_SEMS,)),
        ],
        compiler_params=pltpu.CompilerParams(
            collective_id=0, has_side_effects=True, vmem_limit_bytes=48 * 2**20
        ),
        name="window_gradients",
    )(heat, bias, image_shard, text_shard)


def solution(mesh):
    return jax.shard_map(
        shards,
        mesh=mesh,
        in_specs=(P("tensor", "dp"), P("tensor", "dp"), P(), P()),
        out_specs=(P("tensor", "dp"), P("tensor", "dp")),
        check_vma=False,
    )
```

```python
import jax
import jax.numpy as jnp
from jax import lax
from jax.experimental import pallas as pl
from jax.experimental.pallas import tpu as pltpu
from jax.sharding import PartitionSpec as P

SHIFTS = 4
N_Q = 4
MESH = pl.DeviceIdType.MESH
F32 = jnp.float32
BF16 = jnp.bfloat16

A_DIRECT_P, A_DIRECT_M, A_HALF_P, A_HALF_M, A_ON_P, A_ON_M = range(6)
T_SIB, T_OWN_P, T_OWN_M, T_SIB_P, T_SIB_M, T_ON_P, T_ON_M = range(6, 13)
B_FAR_P, B_FAR_M, B_NEAR_P, B_NEAR_M, B_SUM_P, B_SUM_M, B_SIB = range(13, 20)
E_DIRECT_P, E_DIRECT_M, E_HALF_P, E_HALF_M, E_ON_P, E_ON_M = range(20, 26)
G_SIB = 26
I_SIB = 30
CHAIN = 46
BACK = 58
STOP = 70
LAND = 82
PAUSE = 86
N_SEMS = 90

HALF = 32
BACK_STOP = 29
STOPS = {3: 24, 1: 16, 2: 8, 4: 24, 7: 16, 5: 8, 10: 24, 8: 16, 11: 8}


def split(value):
    high = value.astype(BF16)
    return high, (value - high.astype(F32)).astype(BF16)


def dot3(a_high, a_low, b_high, b_low, dims):
    def one(a, b):
        return lax.dot_general(a, b, (dims, ((), ())), preferred_element_type=F32)

    return one(a_high, b_high) + (one(a_high, b_low) + one(a_low, b_high))


def kernel(
    n_dp,
    heat_ref,
    bias_ref,
    img_ref,
    txt_ref,
    gi_ref,
    gt_ref,
    text,
    image,
    t_high,
    t_low,
    i_high,
    i_low,
    g_text,
    g_image,
    g_other,
    back,
    far_in,
    near_in,
    keep,
    half_in,
    stop,
    landed,
    pause,
    send_sem,
    recv_sem,
):
    d, rows = img_ref.shape
    half, piece = rows // 2, rows // N_Q
    dp, t = lax.axis_index("dp"), lax.axis_index("tensor")
    q, c = t // 2, t % 2
    o = 1 - c
    at = [lax.rem(q + r, N_Q) for r in range(N_Q)]
    sib = (dp, 2 * q + o)
    up, down = (dp, 2 * at[1] + c), (dp, 2 * at[3] + c)
    after, before = (lax.rem(dp + 1, n_dp), t), (lax.rem(dp + n_dp - 1, n_dp), t)
    column = lax.rem(dp, HALF)
    here = dp - column
    there = HALF - here
    started = []

    def remote(index, src, dst, device, landing=None):
        return pltpu.make_async_remote_copy(
            src_ref=src,
            dst_ref=dst,
            send_sem=send_sem.at[index],
            recv_sem=recv_sem.at[index if landing is None else landing],
            device_id=device,
            device_id_type=MESH,
        )

    def send(index, src, dst, device):
        copy = remote(index, src, dst, device)
        copy.start()
        started.append(copy)

    def arrive(index, dst):
        remote(index, dst, dst, sib).wait_recv()

    def member(block, r):
        return (block, 2 * at[r] + c)

    def piece_of(ref, r, first=0, count=None):
        cols = pl.ds(pl.multiple_of(at[r] * piece, piece), piece)
        return ref.at[pl.ds(first, d if count is None else count), cols]

    def half_of(ref, which):
        return ref.at[:, pl.ds(pl.multiple_of(which * half, half), half)]

    barrier = pltpu.get_barrier_semaphore()
    partners = (sib, up, down, after, before)
    for partner in partners:
        pl.semaphore_signal(barrier, inc=1, device_id=partner, device_id_type=MESH)
    greeted = len(partners)
    edge = HALF - 1
    meetings = [(k, there + edge, N_Q) for k in range(SHIFTS - 1)]
    meetings += [(edge, there + k, N_Q) for k in range(SHIFTS - 1)]
    for stop_at in sorted(set(STOPS.values())):
        meetings += [(0, here + stop_at, 1), (stop_at, here, 1)]
        meetings += [(edge, there + stop_at, 1), (stop_at, there + edge, 1)]
    meetings += [(edge, here + BACK_STOP, 1), (BACK_STOP, here + edge, 1)]
    meetings += [(BACK_STOP, there + SHIFTS - 2, N_Q), (SHIFTS - 2, there + BACK_STOP, N_Q)]
    for where, block, count in meetings:

        @pl.when(column == where)
        def _():
            for r in range(count):
                pl.semaphore_signal(
                    barrier, inc=1, device_id=member(block, r), device_id_type=MESH
                )

        greeted += jnp.where(column == where, count, 0)
    pl.semaphore_wait(barrier, greeted)

    h = d // 2
    send(A_HALF_P, piece_of(img_ref, 2, 0, h), half_in.at[0], up)
    send(A_HALF_M, piece_of(img_ref, 2, h, h), half_in.at[1], down)
    image[0, c, q] = piece_of(img_ref, 0)[...]

    inside = []

    def opposite(r):
        return (N_Q - r) % N_Q

    def chain(k, r):
        if k < SHIFTS - 1:
            number = 4 * k + r
            src, dst = image.at[k, c, at[r]], image.at[k + 1, c, at[r]]
            copy = remote(CHAIN + number, src, dst, before)
            started.append(copy)
            if number in STOPS:
                detour = remote(
                    CHAIN + number, src, stop.at[number], (here + STOPS[number], t), STOP + number
                )
                pl.when(column != 0)(copy.start)
                pl.when(column == 0)(detour.start)
            else:
                copy.start()
        send(I_SIB + 4 * k + r, image.at[k, c, at[r]], image.at[k, c, at[r]], sib)

    def chained(k, r):
        arrive(CHAIN + 4 * (k - 1) + r, image.at[k, c, at[r]])
        chain(k, r)

    def pass_edge(k, r):
        number = 4 * (k - 1) + r
        if number in STOPS:
            dst = image.at[k, c, at[r]]
            copy = remote(STOP + number, stop.at[number], dst, (there + edge, t), CHAIN + number)

            @pl.when(column == STOPS[number])
            def _():
                arrive(STOP + number, stop.at[number])
                copy.start()

            inside.append((column == STOPS[number], copy))

    chain(0, 0)
    send(A_DIRECT_P, piece_of(img_ref, 1), image.at[0, c, q], up)
    send(A_DIRECT_M, piece_of(img_ref, 3), image.at[0, c, q], down)
    send(T_SIB, half_of(txt_ref, o), text.at[c, q], sib)
    text[c, q] = half_of(txt_ref, c)[...]

    arrive(A_HALF_P, half_in.at[0])
    send(A_ON_P, half_in.at[0], image.at[0, c, at[3], pl.ds(0, h)], up)
    arrive(A_HALF_M, half_in.at[1])
    send(A_ON_M, half_in.at[1], image.at[0, c, at[1], pl.ds(h, h)], down)
    send(T_OWN_P, text.at[c, q], text.at[c, q], up)
    send(T_OWN_M, text.at[c, q], text.at[c, q], down)

    pass_edge(1, 0)
    chained(1, 0)
    arrive(A_DIRECT_P, image.at[0, c, at[3]])
    chain(0, 3)
    arrive(A_DIRECT_M, image.at[0, c, at[1]])
    chain(0, 1)
    arrive(T_SIB, text.at[o, q])
    send(T_SIB_P, text.at[o, q], text.at[o, q], up)
    send(T_SIB_M, text.at[o, q], text.at[o, q], down)
    arrive(A_ON_P, image.at[0, c, at[2], pl.ds(0, h)])
    arrive(A_ON_M, image.at[0, c, at[2], pl.ds(h, h)])
    chain(0, 2)
    pass_edge(2, 0)
    chained(2, 0)
    pass_edge(1, 3)
    chained(1, 3)
    pass_edge(1, 1)
    chained(1, 1)
    arrive(T_OWN_P, text.at[c, at[3]])
    send(T_ON_P, text.at[c, at[3]], text.at[c, at[3]], up)
    pass_edge(1, 2)
    chained(1, 2)
    pass_edge(3, 0)
    chained(3, 0)
    pass_edge(2, 3)
    chained(2, 3)
    pass_edge(2, 1)
    chained(2, 1)
    pass_edge(2, 2)
    chained(2, 2)
    arrive(T_OWN_M, text.at[c, at[1]])
    arrive(T_SIB_M, text.at[o, at[1]])
    send(T_ON_M, text.at[o, at[1]], text.at[o, at[1]], down)
    for r in (3, 1, 2):
        pass_edge(3, r)

    def text_ready(part, r):
        t_high[part, at[r]], t_low[part, at[r]] = split(text[part, at[r]])

    def image_ready(k, part, r):
        cols = slice(k * piece, (k + 1) * piece)
        i_high[part, at[r], :, cols], i_low[part, at[r], :, cols] = split(image[k, part, at[r]])

    def image_sibling(k, r):
        arrive(I_SIB + 4 * k + r, image.at[k, o, at[r]])
        image_ready(k, o, r)

    text_ready(c, 0)
    text_ready(o, 0)
    text_ready(c, 3)
    text_ready(c, 1)
    text_ready(o, 1)
    for k in range(SHIFTS - 1):
        for r in (0, 3, 1, 2):
            image_ready(k, c, r)
            image_sibling(k, r)
    for r in (3, 1, 2):
        chained(3, r)
    for r in (0, 3, 1, 2):
        image_ready(3, c, r)
        image_sibling(3, r)
    arrive(T_SIB_P, text.at[o, at[3]])
    text_ready(o, 3)
    arrive(T_ON_P, text.at[c, at[2]])
    text_ready(c, 2)
    arrive(T_ON_M, text.at[o, at[2]])
    text_ready(o, 2)

    depth = 2 * N_Q * d
    th, tl = t_high[...].reshape(depth, half), t_low[...].reshape(depth, half)
    ih, il = i_high[...].reshape(depth, rows), i_low[...].reshape(depth, rows)
    dots = dot3(th, tl, ih, il, ((0,), (0,)))
    heat = jnp.exp(jnp.full((1, rows), heat_ref[0], F32))
    slope = jax.nn.sigmoid(heat * dots + bias_ref[0])
    text_id = lax.broadcasted_iota(jnp.int32, slope.shape, 0) + c * half
    image_id = lax.broadcasted_iota(jnp.int32, slope.shape, 1)
    match = (image_id < piece) & (text_id == image_id + q * piece)
    slope = heat * (slope - jnp.where(match, 1.0, 0.0).astype(F32))
    sh, sl = split(slope)

    def image_gradient(ks):
        lo, hi = ks[0] * piece, (ks[-1] + 1) * piece
        grad = dot3(th, tl, sh[:, lo:hi], sl[:, lo:hi], ((1,), (0,)))
        grad = grad.reshape(2, N_Q, d, hi - lo)
        for i, k in enumerate(ks):
            g_image[k] = grad[..., i * piece : (i + 1) * piece]
            send(G_SIB + k, g_image.at[k, o], g_other.at[k], sib)

    def text_gradient(r):
        for part in range(2):
            g_text[part, at[r]] = dot3(
                i_high[part, at[r]], i_low[part, at[r]], sh, sl, ((1,), (1,))
            )

    def add_sibling(k):
        arrive(G_SIB + k, g_other.at[k])
        g_image[k, c] += g_other[k]

    paused = []

    def give_back(step, r, grad):
        copy = remote(BACK + 4 * step + r, grad, back.at[step, at[r]], after)
        pl.when(column != HALF - 1)(copy.start)
        cols = pl.ds(pl.multiple_of(q * piece, piece), piece)
        target = member(there + SHIFTS - 2 - step, r)
        if step == 0:
            leap = remote(BACK + r, grad, pause.at[r], (here + BACK_STOP, t), PAUSE + r)
            onward = remote(PAUSE + r, pause.at[r], landed.at[:, cols], target, LAND + opposite(r))
            paused.append(onward)
        else:
            leap = remote(
                BACK + 4 * step + r, grad, landed.at[:, cols], target, LAND + opposite(r)
            )
        pl.when(column == HALF - 1)(leap.start)
        started.append(copy)

    def returned(step, r):
        slot = back.at[step, at[r]]
        pl.when(column != 0)(remote(BACK + 4 * step + r, slot, slot, sib).wait_recv)
        slot[...] += g_image[2 - step, c, at[r]]

    @pl.when(column == 0)
    def _():
        back[...] = jnp.zeros_like(back)

    order = (2, 1, 3, 0)
    image_gradient((2, 3))
    text_gradient(2)
    send(B_FAR_P, g_text.at[0, at[2]], far_in.at[0], up)
    send(B_FAR_M, g_text.at[1, at[2]], far_in.at[1], down)
    add_sibling(3)
    for r in order:
        give_back(0, r, g_image.at[3, c, at[r]])
    text_gradient(1)
    send(B_NEAR_P, g_text.at[1, at[1]], near_in.at[0], up)
    text_gradient(3)
    send(B_NEAR_M, g_text.at[0, at[3]], near_in.at[1], down)
    image_gradient((0, 1))

    @pl.when(column == BACK_STOP)
    def _():
        for i, r in enumerate(order):
            arrive(PAUSE + r, pause.at[r])
            paused[i].start()

    inside.extend((column == BACK_STOP, copy) for copy in paused)
    add_sibling(2)
    text_gradient(0)
    for r in order:
        returned(0, r)
        give_back(1, r, back.at[0, at[r]])
    add_sibling(1)
    add_sibling(0)
    arrive(B_FAR_P, far_in.at[0])
    g_text[0, at[1]] += far_in[0]
    send(B_SUM_P, g_text.at[0, at[1]], near_in.at[2], up)
    arrive(B_FAR_M, far_in.at[1])
    g_text[1, at[3]] += far_in[1]
    send(B_SUM_M, g_text.at[1, at[3]], near_in.at[3], down)
    for r in order:
        returned(1, r)
        give_back(2, r, back.at[1, at[r]])

    arrive(B_NEAR_P, near_in.at[0])
    arrive(B_NEAR_M, near_in.at[1])
    arrive(B_SUM_P, near_in.at[2])
    arrive(B_SUM_M, near_in.at[3])
    g_text[0, q] += near_in[1] + near_in[2]
    g_text[1, q] += near_in[0] + near_in[3]
    keep[...] = g_text[o, q]
    send(B_SIB, keep, half_of(gt_ref, c), sib)
    half_of(gt_ref, c)[...] = g_text[c, q]

    def own_columns(r, first=0, count=None):
        return piece_of(gi_ref, r, first, count)

    returned(2, 2)
    send(E_HALF_P, back.at[2, at[2], pl.ds(0, h)], half_in.at[2], up)
    send(E_HALF_M, back.at[2, at[2], pl.ds(h, h)], half_in.at[3], down)
    returned(2, 1)
    send(E_DIRECT_P, back.at[2, at[1]], own_columns(0), up)
    returned(2, 3)
    send(E_DIRECT_M, back.at[2, at[3]], own_columns(0), down)
    arrive(E_HALF_P, half_in.at[2])
    send(E_ON_P, half_in.at[2], own_columns(3, 0, h), up)
    arrive(E_HALF_M, half_in.at[3])
    send(E_ON_M, half_in.at[3], own_columns(1, h, h), down)
    returned(2, 0)
    own_columns(0)[...] = back[2, q]
    arrive(E_DIRECT_P, own_columns(3))
    arrive(E_DIRECT_M, own_columns(1))
    arrive(E_ON_P, own_columns(2, 0, h))
    arrive(E_ON_M, own_columns(2, h, h))
    arrive(B_SIB, half_of(gt_ref, o))

    @pl.when(column < SHIFTS - 1)
    def _():
        for r in range(N_Q):
            arrive(LAND + r, piece_of(landed, r))
        gi_ref[...] += landed[...]

    for copy in started:
        copy.wait_send()
    for guard, copy in inside:
        pl.when(guard)(copy.wait_send)


def shards(image_shard, text_shard, heat, bias):
    d, rows = image_shard.shape
    half, piece = rows // 2, rows // N_Q
    vmem = pl.BlockSpec(memory_space=pltpu.VMEM)
    smem = pl.BlockSpec(memory_space=pltpu.SMEM)
    n_dp = lax.axis_size("dp")

    def body(*refs):
        kernel(n_dp, *refs)

    return pl.pallas_call(
        body,
        out_shape=(jax.ShapeDtypeStruct((d, rows), F32), jax.ShapeDtypeStruct((d, rows), F32)),
        in_specs=[smem, smem, vmem, vmem],
        out_specs=(vmem, vmem),
        scratch_shapes=[
            pltpu.VMEM((2, N_Q, d, half), F32),
            pltpu.VMEM((SHIFTS, 2, N_Q, d, piece), F32),
            pltpu.VMEM((2, N_Q, d, half), BF16),
            pltpu.VMEM((2, N_Q, d, half), BF16),
            pltpu.VMEM((2, N_Q, d, rows), BF16),
            pltpu.VMEM((2, N_Q, d, rows), BF16),
            pltpu.VMEM((2, N_Q, d, half), F32),
            pltpu.VMEM((SHIFTS, 2, N_Q, d, piece), F32),
            pltpu.VMEM((SHIFTS, N_Q, d, piece), F32),
            pltpu.VMEM((SHIFTS - 1, N_Q, d, piece), F32),
            pltpu.VMEM((2, d, half), F32),
            pltpu.VMEM((4, d, half), F32),
            pltpu.VMEM((d, half), F32),
            pltpu.VMEM((4, d // 2, piece), F32),
            pltpu.VMEM((4 * (SHIFTS - 1), d, piece), F32),
            pltpu.VMEM((d, rows), F32),
            pltpu.VMEM((N_Q, d, piece), F32),
            pltpu.SemaphoreType.DMA((N_SEMS,)),
            pltpu.SemaphoreType.DMA((N_SEMS,)),
        ],
        compiler_params=pltpu.CompilerParams(
            collective_id=0, has_side_effects=True, vmem_limit_bytes=48 * 2**20
        ),
        name="window_gradients",
    )(heat, bias, image_shard, text_shard)


def solution(mesh):
    return jax.shard_map(
        shards,
        mesh=mesh,
        in_specs=(P("tensor", "dp"), P("tensor", "dp"), P(), P()),
        out_specs=(P("tensor", "dp"), P("tensor", "dp")),
        check_vma=False,
    )
```

```python
import jax
import jax.numpy as jnp
from jax import lax
from jax.experimental import pallas as pl
from jax.experimental.pallas import tpu as pltpu
from jax.sharding import PartitionSpec as P

SHIFTS = 4
N_Q = 4
MESH = pl.DeviceIdType.MESH
F32 = jnp.float32
BF16 = jnp.bfloat16

A_DIRECT_P, A_DIRECT_M, A_HALF_P, A_HALF_M, A_ON_P, A_ON_M = range(6)
T_SIB, T_OWN_P, T_OWN_M, T_SIB_P, T_SIB_M, T_ON_P, T_ON_M = range(6, 13)
B_FAR_P, B_FAR_M, B_NEAR_P, B_NEAR_M, B_SUM_P, B_SUM_M, B_SIB = range(13, 20)
E_DIRECT_P, E_DIRECT_M, E_HALF_P, E_HALF_M, E_ON_P, E_ON_M = range(20, 26)
G_SIB = 26
I_SIB = 30
CHAIN = 46
BACK = 58
STOP = 70
LAND = 82
PAUSE = 86
N_SEMS = 98

HALF = 32
BACK_STOPS = {1: 7, 3: 23, 0: 23, 5: 7, 7: 23, 4: 7, 9: 7, 8: 23}
STOPS = {0: 24, 3: 16, 1: 8, 2: 24, 4: 16, 7: 8, 5: 24, 8: 16, 11: 8}


def split(value):
    high = value.astype(BF16)
    return high, (value - high.astype(F32)).astype(BF16)


def dot3(a_high, a_low, b_high, b_low, dims):
    def one(a, b):
        return lax.dot_general(a, b, (dims, ((), ())), preferred_element_type=F32)

    return one(a_high, b_high) + (one(a_high, b_low) + one(a_low, b_high))


def kernel(
    n_dp,
    heat_ref,
    bias_ref,
    img_ref,
    txt_ref,
    gi_ref,
    gt_ref,
    text,
    image,
    t_high,
    t_low,
    i_high,
    i_low,
    g_text,
    g_image,
    g_other,
    back,
    far_in,
    near_in,
    keep,
    half_in,
    dots,
    stop,
    landed,
    pause,
    send_sem,
    recv_sem,
    local_sem,
):
    d, rows = img_ref.shape
    half, piece = rows // 2, rows // N_Q
    dp, t = lax.axis_index("dp"), lax.axis_index("tensor")
    q, c = t // 2, t % 2
    o = 1 - c
    at = [lax.rem(q + r, N_Q) for r in range(N_Q)]
    sib = (dp, 2 * q + o)
    up, down = (dp, 2 * at[1] + c), (dp, 2 * at[3] + c)
    after, before = (lax.rem(dp + 1, n_dp), t), (lax.rem(dp + n_dp - 1, n_dp), t)
    column = lax.rem(dp, HALF)
    here = dp - column
    there = HALF - here
    started = []

    def remote(index, src, dst, device, landing=None):
        return pltpu.make_async_remote_copy(
            src_ref=src,
            dst_ref=dst,
            send_sem=send_sem.at[index],
            recv_sem=recv_sem.at[index if landing is None else landing],
            device_id=device,
            device_id_type=MESH,
        )

    def send(index, src, dst, device):
        copy = remote(index, src, dst, device)
        copy.start()
        started.append(copy)

    def arrive(index, dst):
        remote(index, dst, dst, sib).wait_recv()

    def member(block, r):
        return (block, 2 * at[r] + c)

    def piece_of(ref, r, first=0, count=None):
        cols = pl.ds(pl.multiple_of(at[r] * piece, piece), piece)
        return ref.at[pl.ds(first, d if count is None else count), cols]

    def half_of(ref, which):
        return ref.at[:, pl.ds(pl.multiple_of(which * half, half), half)]

    own_piece = pltpu.make_async_copy(piece_of(img_ref, 0), image.at[0, c, q], local_sem.at[0])
    own_text = pltpu.make_async_copy(half_of(txt_ref, c), text.at[c, q], local_sem.at[1])
    own_piece.start()
    own_text.start()
    barrier = pltpu.get_barrier_semaphore()
    partners = (sib, up, down, after, before)
    for partner in partners:
        pl.semaphore_signal(barrier, inc=1, device_id=partner, device_id_type=MESH)
    greeted = len(partners)
    edge = HALF - 1
    meetings = [(k, there + edge, N_Q) for k in range(SHIFTS - 1)]
    meetings += [(edge, there + k, N_Q) for k in range(SHIFTS - 1)]
    for stop_at in sorted(set(STOPS.values())):
        meetings += [(0, here + stop_at, 1), (stop_at, here, 1)]
        meetings += [(edge, there + stop_at, 1), (stop_at, there + edge, 1)]
    for stop_at in sorted(set(BACK_STOPS.values())):
        meetings += [(edge, here + stop_at, 1), (stop_at, here + edge, 1)]
        for k in range(SHIFTS - 1):
            meetings += [(stop_at, there + k, N_Q), (k, there + stop_at, N_Q)]
    for where, block, count in meetings:

        @pl.when(column == where)
        def _():
            for r in range(count):
                pl.semaphore_signal(
                    barrier, inc=1, device_id=member(block, r), device_id_type=MESH
                )

        greeted += jnp.where(column == where, count, 0)
    pl.semaphore_wait(barrier, greeted)

    h = d // 2
    send(A_HALF_P, piece_of(img_ref, 2, 0, h), half_in.at[0], up)
    send(A_HALF_M, piece_of(img_ref, 2, h, h), half_in.at[1], down)

    inside = []

    def opposite(r):
        return (N_Q - r) % N_Q

    def chain(k, r):
        if k < SHIFTS - 1:
            number = 4 * k + r
            src, dst = image.at[k, c, at[r]], image.at[k + 1, c, at[r]]
            copy = remote(CHAIN + number, src, dst, before)
            started.append(copy)
            if number in STOPS:
                detour = remote(
                    CHAIN + number, src, stop.at[number], (here + STOPS[number], t), STOP + number
                )
                pl.when(column != 0)(copy.start)
                pl.when(column == 0)(detour.start)
            else:
                copy.start()
        send(I_SIB + 4 * k + r, image.at[k, c, at[r]], image.at[k, c, at[r]], sib)

    def chained(k, r):
        arrive(CHAIN + 4 * (k - 1) + r, image.at[k, c, at[r]])
        chain(k, r)

    def pass_edge(k, r):
        number = 4 * (k - 1) + r
        if number in STOPS:
            dst = image.at[k, c, at[r]]
            copy = remote(STOP + number, stop.at[number], dst, (there + edge, t), CHAIN + number)

            @pl.when(column == STOPS[number])
            def _():
                arrive(STOP + number, stop.at[number])
                copy.start()

            inside.append((column == STOPS[number], copy))

    own_piece.wait()
    chain(0, 0)
    send(A_DIRECT_P, piece_of(img_ref, 1), image.at[0, c, q], up)
    send(A_DIRECT_M, piece_of(img_ref, 3), image.at[0, c, q], down)
    send(T_SIB, half_of(txt_ref, o), text.at[c, q], sib)

    arrive(A_HALF_P, half_in.at[0])
    send(A_ON_P, half_in.at[0], image.at[0, c, at[3], pl.ds(0, h)], up)
    arrive(A_HALF_M, half_in.at[1])
    send(A_ON_M, half_in.at[1], image.at[0, c, at[1], pl.ds(h, h)], down)
    own_text.wait()
    send(T_OWN_P, text.at[c, q], text.at[c, q], up)
    send(T_OWN_M, text.at[c, q], text.at[c, q], down)

    pass_edge(1, 0)
    chained(1, 0)
    arrive(A_DIRECT_P, image.at[0, c, at[3]])
    chain(0, 3)
    arrive(A_DIRECT_M, image.at[0, c, at[1]])
    chain(0, 1)
    arrive(T_SIB, text.at[o, q])
    send(T_SIB_P, text.at[o, q], text.at[o, q], up)
    send(T_SIB_M, text.at[o, q], text.at[o, q], down)
    arrive(A_ON_P, image.at[0, c, at[2], pl.ds(0, h)])
    arrive(A_ON_M, image.at[0, c, at[2], pl.ds(h, h)])
    chain(0, 2)
    pass_edge(2, 0)
    chained(2, 0)
    pass_edge(1, 3)
    chained(1, 3)
    pass_edge(1, 1)
    chained(1, 1)
    arrive(T_OWN_P, text.at[c, at[3]])
    send(T_ON_P, text.at[c, at[3]], text.at[c, at[3]], up)
    pass_edge(1, 2)
    chained(1, 2)
    pass_edge(3, 0)
    chained(3, 0)
    pass_edge(2, 3)
    chained(2, 3)
    pass_edge(2, 1)
    chained(2, 1)
    pass_edge(2, 2)
    chained(2, 2)
    arrive(T_OWN_M, text.at[c, at[1]])
    arrive(T_SIB_M, text.at[o, at[1]])
    send(T_ON_M, text.at[o, at[1]], text.at[o, at[1]], down)
    for r in (3, 1, 2):
        pass_edge(3, r)

    def text_ready(part, r):
        t_high[part, at[r]], t_low[part, at[r]] = split(text[part, at[r]])

    def image_ready(k, part, r):
        cols = slice(k * piece, (k + 1) * piece)
        i_high[part, at[r], :, cols], i_low[part, at[r], :, cols] = split(image[k, part, at[r]])

    def image_sibling(k, r):
        arrive(I_SIB + 4 * k + r, image.at[k, o, at[r]])
        image_ready(k, o, r)

    text_ready(c, 0)
    text_ready(o, 0)
    text_ready(c, 3)
    text_ready(c, 1)
    text_ready(o, 1)
    for k in range(SHIFTS - 1):
        for r in (0, 3, 1, 2):
            image_ready(k, c, r)
            image_sibling(k, r)
    for r in (3, 1, 2):
        chained(3, r)
    for r in (0, 3, 1, 2):
        image_ready(3, c, r)
        image_sibling(3, r)
    arrive(T_SIB_P, text.at[o, at[3]])
    text_ready(o, 3)

    def quarter_dots(r):
        def rows_of(ref):
            return ref[:, at[r]].reshape(2 * d, ref.shape[-1])

        return dot3(
            rows_of(t_high), rows_of(t_low), rows_of(i_high), rows_of(i_low), ((0,), (0,))
        )

    dots[...] = quarter_dots(0) + quarter_dots(3) + quarter_dots(1)
    arrive(T_ON_P, text.at[c, at[2]])
    text_ready(c, 2)
    arrive(T_ON_M, text.at[o, at[2]])
    text_ready(o, 2)

    depth = 2 * N_Q * d
    th, tl = t_high[...].reshape(depth, half), t_low[...].reshape(depth, half)
    heat = jnp.exp(jnp.full((1, rows), heat_ref[0], F32))
    slope = jax.nn.sigmoid(heat * (dots[...] + quarter_dots(2)) + bias_ref[0])
    text_id = lax.broadcasted_iota(jnp.int32, slope.shape, 0) + c * half
    image_id = lax.broadcasted_iota(jnp.int32, slope.shape, 1)
    match = (image_id < piece) & (text_id == image_id + q * piece)
    slope = heat * (slope - jnp.where(match, 1.0, 0.0).astype(F32))
    sh, sl = split(slope)

    def image_gradient(ks):
        lo, hi = ks[0] * piece, (ks[-1] + 1) * piece
        grad = dot3(th, tl, sh[:, lo:hi], sl[:, lo:hi], ((1,), (0,)))
        grad = grad.reshape(2, N_Q, d, hi - lo)
        for i, k in enumerate(ks):
            g_image[k] = grad[..., i * piece : (i + 1) * piece]
            send(G_SIB + k, g_image.at[k, o], g_other.at[k], sib)

    def text_gradient(r):
        for part in range(2):
            g_text[part, at[r]] = dot3(
                i_high[part, at[r]], i_low[part, at[r]], sh, sl, ((1,), (1,))
            )

    def add_sibling(k):
        arrive(G_SIB + k, g_other.at[k])
        g_image[k, c] += g_other[k]

    paused = {}

    def give_on(step):
        for r in order:
            number = 4 * step + r
            if number in BACK_STOPS:

                @pl.when(column == BACK_STOPS[number])
                def _():
                    arrive(PAUSE + number, pause.at[number])
                    paused[number].start()

    def give_back(step, r, grad):
        copy = remote(BACK + 4 * step + r, grad, back.at[step, at[r]], after)
        pl.when(column != HALF - 1)(copy.start)
        cols = pl.ds(pl.multiple_of(q * piece, piece), piece)
        target = member(there + SHIFTS - 2 - step, r)
        number = 4 * step + r
        if number in BACK_STOPS:
            leap = remote(
                BACK + number, grad, pause.at[number], (here + BACK_STOPS[number], t), PAUSE + number
            )
            onward = remote(
                PAUSE + number, pause.at[number], landed.at[:, cols], target, LAND + opposite(r)
            )
            paused[number] = onward
            inside.append((column == BACK_STOPS[number], onward))
        else:
            leap = remote(BACK + number, grad, landed.at[:, cols], target, LAND + opposite(r))
        pl.when(column == HALF - 1)(leap.start)
        started.append(copy)

    def returned(step, r):
        slot = back.at[step, at[r]]
        pl.when(column != 0)(remote(BACK + 4 * step + r, slot, slot, sib).wait_recv)
        slot[...] += g_image[2 - step, c, at[r]]

    @pl.when(column == 0)
    def _():
        back[...] = jnp.zeros_like(back)

    order = (2, 1, 3, 0)
    image_gradient((3,))
    text_gradient(2)
    send(B_FAR_P, g_text.at[0, at[2]], far_in.at[0], up)
    send(B_FAR_M, g_text.at[1, at[2]], far_in.at[1], down)
    add_sibling(3)
    for r in order:
        give_back(0, r, g_image.at[3, c, at[r]])
    text_gradient(1)
    send(B_NEAR_P, g_text.at[1, at[1]], near_in.at[0], up)
    text_gradient(3)
    send(B_NEAR_M, g_text.at[0, at[3]], near_in.at[1], down)
    image_gradient((2,))
    image_gradient((0, 1))
    add_sibling(2)
    text_gradient(0)
    for r in order:
        returned(0, r)
        give_back(1, r, back.at[0, at[r]])
    add_sibling(1)
    add_sibling(0)
    arrive(B_FAR_P, far_in.at[0])
    g_text[0, at[1]] += far_in[0]
    send(B_SUM_P, g_text.at[0, at[1]], near_in.at[2], up)
    arrive(B_FAR_M, far_in.at[1])
    g_text[1, at[3]] += far_in[1]
    send(B_SUM_M, g_text.at[1, at[3]], near_in.at[3], down)
    for r in order:
        returned(1, r)
        give_back(2, r, back.at[1, at[r]])
    give_on(0)

    arrive(B_NEAR_P, near_in.at[0])
    arrive(B_NEAR_M, near_in.at[1])
    arrive(B_SUM_P, near_in.at[2])
    arrive(B_SUM_M, near_in.at[3])
    g_text[0, q] += near_in[1] + near_in[2]
    g_text[1, q] += near_in[0] + near_in[3]
    keep[...] = g_text[o, q]
    send(B_SIB, keep, half_of(gt_ref, c), sib)
    half_of(gt_ref, c)[...] = g_text[c, q]
    give_on(1)

    def own_columns(r, first=0, count=None):
        return piece_of(gi_ref, r, first, count)

    returned(2, 2)
    send(E_HALF_P, back.at[2, at[2], pl.ds(0, h)], half_in.at[2], up)
    send(E_HALF_M, back.at[2, at[2], pl.ds(h, h)], half_in.at[3], down)
    returned(2, 1)
    send(E_DIRECT_P, back.at[2, at[1]], own_columns(0), up)
    returned(2, 3)
    send(E_DIRECT_M, back.at[2, at[3]], own_columns(0), down)
    arrive(E_HALF_P, half_in.at[2])
    send(E_ON_P, half_in.at[2], own_columns(3, 0, h), up)
    arrive(E_HALF_M, half_in.at[3])
    send(E_ON_M, half_in.at[3], own_columns(1, h, h), down)
    returned(2, 0)
    own_columns(0)[...] = back[2, q]
    give_on(2)
    arrive(E_DIRECT_P, own_columns(3))
    arrive(E_DIRECT_M, own_columns(1))
    arrive(E_ON_P, own_columns(2, 0, h))
    arrive(E_ON_M, own_columns(2, h, h))
    arrive(B_SIB, half_of(gt_ref, o))

    @pl.when(column < SHIFTS - 1)
    def _():
        for r in range(N_Q):
            arrive(LAND + r, piece_of(landed, r))
        gi_ref[...] += landed[...]

    for copy in started:
        copy.wait_send()
    for guard, copy in inside:
        pl.when(guard)(copy.wait_send)


def shards(image_shard, text_shard, heat, bias):
    d, rows = image_shard.shape
    half, piece = rows // 2, rows // N_Q
    vmem = pl.BlockSpec(memory_space=pltpu.VMEM)
    smem = pl.BlockSpec(memory_space=pltpu.SMEM)
    hbm = pl.BlockSpec(memory_space=pl.ANY)
    n_dp = lax.axis_size("dp")

    def body(*refs):
        kernel(n_dp, *refs)

    return pl.pallas_call(
        body,
        out_shape=(jax.ShapeDtypeStruct((d, rows), F32), jax.ShapeDtypeStruct((d, rows), F32)),
        in_specs=[smem, smem, hbm, hbm],
        out_specs=(vmem, vmem),
        scratch_shapes=[
            pltpu.VMEM((2, N_Q, d, half), F32),
            pltpu.VMEM((SHIFTS, 2, N_Q, d, piece), F32),
            pltpu.VMEM((2, N_Q, d, half), BF16),
            pltpu.VMEM((2, N_Q, d, half), BF16),
            pltpu.VMEM((2, N_Q, d, rows), BF16),
            pltpu.VMEM((2, N_Q, d, rows), BF16),
            pltpu.VMEM((2, N_Q, d, half), F32),
            pltpu.VMEM((SHIFTS, 2, N_Q, d, piece), F32),
            pltpu.VMEM((SHIFTS, N_Q, d, piece), F32),
            pltpu.VMEM((SHIFTS - 1, N_Q, d, piece), F32),
            pltpu.VMEM((2, d, half), F32),
            pltpu.VMEM((4, d, half), F32),
            pltpu.VMEM((d, half), F32),
            pltpu.VMEM((4, d // 2, piece), F32),
            pltpu.VMEM((half, rows), F32),
            pltpu.VMEM((4 * (SHIFTS - 1), d, piece), F32),
            pltpu.VMEM((d, rows), F32),
            pltpu.VMEM((4 * (SHIFTS - 1), d, piece), F32),
            pltpu.SemaphoreType.DMA((N_SEMS,)),
            pltpu.SemaphoreType.DMA((N_SEMS,)),
            pltpu.SemaphoreType.DMA((2,)),
        ],
        compiler_params=pltpu.CompilerParams(
            collective_id=0, has_side_effects=True, vmem_limit_bytes=48 * 2**20
        ),
        name="window_gradients",
    )(heat, bias, image_shard, text_shard)


def solution(mesh):
    return jax.shard_map(
        shards,
        mesh=mesh,
        in_specs=(P("tensor", "dp"), P("tensor", "dp"), P(), P()),
        out_specs=(P("tensor", "dp"), P("tensor", "dp")),
        check_vma=False,
    )
```

```python
import jax
import jax.numpy as jnp
from jax import lax
from jax.experimental import pallas as pl
from jax.experimental.pallas import tpu as pltpu
from jax.sharding import PartitionSpec as P

SHIFTS = 4
N_Q = 4
MESH = pl.DeviceIdType.MESH
F32 = jnp.float32
BF16 = jnp.bfloat16

A_DIRECT_P, A_DIRECT_M, A_HALF_P, A_HALF_M, A_ON_P, A_ON_M = range(6)
T_SIB, T_OWN_P, T_OWN_M, T_SIB_P, T_SIB_M, T_ON_P, T_ON_M = range(6, 13)
B_FAR_P, B_FAR_M, B_NEAR_P, B_NEAR_M, B_SUM_P, B_SUM_M, B_SIB = range(13, 20)
E_DIRECT_P, E_DIRECT_M, E_HALF_P, E_HALF_M, E_ON_P, E_ON_M = range(20, 26)
G_SIB = 26
I_SIB = 30
CHAIN = 46
BACK = 58
STOP = 70
LAND = 82
PAUSE = 86
N_SEMS = 98

HALF = 32
BACK_STOPS = {1: 7, 3: 23, 0: 23, 5: 7, 7: 23, 4: 7, 9: 7, 8: 23}
STOPS = {0: 24, 3: 16, 1: 8, 2: 24, 4: 16, 7: 8, 5: 24, 8: 16, 11: 8}


def split(value):
    high = value.astype(BF16)
    return high, (value - high.astype(F32)).astype(BF16)


def dot3(a_high, a_low, b_high, b_low, dims):
    def one(a, b):
        return lax.dot_general(a, b, (dims, ((), ())), preferred_element_type=F32)

    return one(a_high, b_high) + (one(a_high, b_low) + one(a_low, b_high))


def kernel(
    n_dp,
    heat_ref,
    bias_ref,
    img_ref,
    txt_ref,
    gi_ref,
    gt_ref,
    text,
    image,
    t_high,
    t_low,
    i_high,
    i_low,
    g_text,
    g_image,
    g_other,
    back,
    far_in,
    near_in,
    keep,
    half_in,
    dots,
    stop,
    landed,
    pause,
    send_sem,
    recv_sem,
    local_sem,
):
    d, rows = img_ref.shape
    half, piece = rows // 2, rows // N_Q
    dp, t = lax.axis_index("dp"), lax.axis_index("tensor")
    q, c = t // 2, t % 2
    o = 1 - c
    at = [lax.rem(q + r, N_Q) for r in range(N_Q)]
    sib = (dp, 2 * q + o)
    up, down = (dp, 2 * at[1] + c), (dp, 2 * at[3] + c)
    after, before = (lax.rem(dp + 1, n_dp), t), (lax.rem(dp + n_dp - 1, n_dp), t)
    column = lax.rem(dp, HALF)
    here = dp - column
    there = HALF - here
    started = []

    def remote(index, src, dst, device, landing=None):
        return pltpu.make_async_remote_copy(
            src_ref=src,
            dst_ref=dst,
            send_sem=send_sem.at[index],
            recv_sem=recv_sem.at[index if landing is None else landing],
            device_id=device,
            device_id_type=MESH,
        )

    def send(index, src, dst, device):
        copy = remote(index, src, dst, device)
        copy.start()
        started.append(copy)

    def arrive(index, dst):
        remote(index, dst, dst, sib).wait_recv()

    def member(block, r):
        return (block, 2 * at[r] + c)

    def piece_of(ref, r, first=0, count=None):
        cols = pl.ds(pl.multiple_of(at[r] * piece, piece), piece)
        return ref.at[pl.ds(first, d if count is None else count), cols]

    def half_of(ref, which):
        return ref.at[:, pl.ds(pl.multiple_of(which * half, half), half)]

    own_piece = pltpu.make_async_copy(piece_of(img_ref, 0), image.at[0, c, q], local_sem.at[0])
    own_text = pltpu.make_async_copy(half_of(txt_ref, c), text.at[c, q], local_sem.at[1])
    own_piece.start()
    own_text.start()
    barrier = pltpu.get_barrier_semaphore()
    partners = (sib, up, down, after, before)
    for partner in partners:
        pl.semaphore_signal(barrier, inc=1, device_id=partner, device_id_type=MESH)
    greeted = len(partners)
    edge = HALF - 1
    meetings = [(k, there + edge, N_Q) for k in range(SHIFTS - 1)]
    meetings += [(edge, there + k, N_Q) for k in range(SHIFTS - 1)]
    for stop_at in sorted(set(STOPS.values())):
        meetings += [(0, here + stop_at, 1), (stop_at, here, 1)]
        meetings += [(edge, there + stop_at, 1), (stop_at, there + edge, 1)]
    for stop_at in sorted(set(BACK_STOPS.values())):
        meetings += [(edge, here + stop_at, 1), (stop_at, here + edge, 1)]
        for k in range(SHIFTS - 1):
            meetings += [(stop_at, there + k, N_Q), (k, there + stop_at, N_Q)]
    for where, block, count in meetings:

        @pl.when(column == where)
        def _():
            for r in range(count):
                pl.semaphore_signal(
                    barrier, inc=1, device_id=member(block, r), device_id_type=MESH
                )

        greeted += jnp.where(column == where, count, 0)
    pl.semaphore_wait(barrier, greeted)

    h = d // 2
    send(A_HALF_P, piece_of(img_ref, 2, 0, h), half_in.at[0], up)
    send(A_HALF_M, piece_of(img_ref, 2, h, h), half_in.at[1], down)

    inside = []

    def opposite(r):
        return (N_Q - r) % N_Q

    def chain(k, r):
        if k < SHIFTS - 1:
            number = 4 * k + r
            src, dst = image.at[k, c, at[r]], image.at[k + 1, c, at[r]]
            copy = remote(CHAIN + number, src, dst, before)
            started.append(copy)
            if number in STOPS:
                detour = remote(
                    CHAIN + number, src, stop.at[number], (here + STOPS[number], t), STOP + number
                )
                pl.when(column != 0)(copy.start)
                pl.when(column == 0)(detour.start)
            else:
                copy.start()
        send(I_SIB + 4 * k + r, image.at[k, c, at[r]], image.at[k, c, at[r]], sib)

    def chained(k, r):
        arrive(CHAIN + 4 * (k - 1) + r, image.at[k, c, at[r]])
        chain(k, r)

    def pass_edge(k, r):
        number = 4 * (k - 1) + r
        if number in STOPS:
            dst = image.at[k, c, at[r]]
            copy = remote(STOP + number, stop.at[number], dst, (there + edge, t), CHAIN + number)

            @pl.when(column == STOPS[number])
            def _():
                arrive(STOP + number, stop.at[number])
                copy.start()

            inside.append((column == STOPS[number], copy))

    own_piece.wait()
    chain(0, 0)
    send(A_DIRECT_P, piece_of(img_ref, 1), image.at[0, c, q], up)
    send(A_DIRECT_M, piece_of(img_ref, 3), image.at[0, c, q], down)
    send(T_SIB, half_of(txt_ref, o), text.at[c, q], sib)

    arrive(A_HALF_P, half_in.at[0])
    send(A_ON_P, half_in.at[0], image.at[0, c, at[3], pl.ds(0, h)], up)
    arrive(A_HALF_M, half_in.at[1])
    send(A_ON_M, half_in.at[1], image.at[0, c, at[1], pl.ds(h, h)], down)
    own_text.wait()
    send(T_OWN_P, text.at[c, q], text.at[c, q], up)
    send(T_OWN_M, text.at[c, q], text.at[c, q], down)

    pass_edge(1, 0)
    chained(1, 0)
    arrive(A_DIRECT_P, image.at[0, c, at[3]])
    chain(0, 3)
    arrive(A_DIRECT_M, image.at[0, c, at[1]])
    chain(0, 1)
    arrive(T_SIB, text.at[o, q])
    send(T_SIB_P, text.at[o, q], text.at[o, q], up)
    send(T_SIB_M, text.at[o, q], text.at[o, q], down)
    arrive(A_ON_P, image.at[0, c, at[2], pl.ds(0, h)])
    arrive(A_ON_M, image.at[0, c, at[2], pl.ds(h, h)])
    chain(0, 2)
    pass_edge(2, 0)
    chained(2, 0)
    pass_edge(1, 3)
    chained(1, 3)
    pass_edge(1, 1)
    chained(1, 1)
    arrive(T_OWN_P, text.at[c, at[3]])
    send(T_ON_P, text.at[c, at[3]], text.at[c, at[3]], up)
    pass_edge(1, 2)
    chained(1, 2)
    pass_edge(3, 0)
    chained(3, 0)
    pass_edge(2, 3)
    chained(2, 3)
    pass_edge(2, 1)
    chained(2, 1)
    pass_edge(2, 2)
    chained(2, 2)
    arrive(T_OWN_M, text.at[c, at[1]])
    arrive(T_SIB_M, text.at[o, at[1]])
    send(T_ON_M, text.at[o, at[1]], text.at[o, at[1]], down)
    for r in (3, 1, 2):
        pass_edge(3, r)

    def text_ready(part, r):
        t_high[part, at[r]], t_low[part, at[r]] = split(text[part, at[r]])

    def image_ready(k, part, r):
        cols = slice(k * piece, (k + 1) * piece)
        i_high[part, at[r], :, cols], i_low[part, at[r], :, cols] = split(image[k, part, at[r]])

    def image_sibling(k, r):
        arrive(I_SIB + 4 * k + r, image.at[k, o, at[r]])
        image_ready(k, o, r)

    text_ready(c, 0)
    text_ready(o, 0)
    text_ready(c, 3)
    text_ready(c, 1)
    text_ready(o, 1)
    for k in range(SHIFTS - 1):
        for r in (0, 3, 1, 2):
            image_ready(k, c, r)
            image_sibling(k, r)
    for r in (3, 1, 2):
        chained(3, r)
    for r in (0, 3, 1, 2):
        image_ready(3, c, r)
        image_sibling(3, r)
    arrive(T_SIB_P, text.at[o, at[3]])
    text_ready(o, 3)

    def quarter_dots(r):
        def rows_of(ref):
            return ref[:, at[r]].reshape(2 * d, ref.shape[-1])

        return dot3(
            rows_of(t_high), rows_of(t_low), rows_of(i_high), rows_of(i_low), ((0,), (0,))
        )

    dots[...] = quarter_dots(0) + quarter_dots(3) + quarter_dots(1)
    arrive(T_ON_P, text.at[c, at[2]])
    text_ready(c, 2)
    arrive(T_ON_M, text.at[o, at[2]])
    text_ready(o, 2)

    depth = 2 * N_Q * d
    th, tl = t_high[...].reshape(depth, half), t_low[...].reshape(depth, half)
    heat = jnp.exp(jnp.full((1, rows), heat_ref[0], F32))
    slope = jax.nn.sigmoid(heat * (dots[...] + quarter_dots(2)) + bias_ref[0])
    text_id = lax.broadcasted_iota(jnp.int32, slope.shape, 0) + c * half
    image_id = lax.broadcasted_iota(jnp.int32, slope.shape, 1)
    match = (image_id < piece) & (text_id == image_id + q * piece)
    slope = heat * (slope - jnp.where(match, 1.0, 0.0).astype(F32))
    sh, sl = split(slope)

    def image_gradient(ks):
        lo, hi = ks[0] * piece, (ks[-1] + 1) * piece
        grad = dot3(th, tl, sh[:, lo:hi], sl[:, lo:hi], ((1,), (0,)))
        grad = grad.reshape(2, N_Q, d, hi - lo)
        for i, k in enumerate(ks):
            g_image[k] = grad[..., i * piece : (i + 1) * piece]
            send(G_SIB + k, g_image.at[k, o], g_other.at[k], sib)

    def text_gradient(r):
        high, low = (ref[:, at[r]].reshape(2 * d, rows) for ref in (i_high, i_low))
        g_text[:, at[r]] = dot3(high, low, sh_t, sl_t, ((1,), (0,))).reshape(2, d, half)

    def add_sibling(k):
        arrive(G_SIB + k, g_other.at[k])
        g_image[k, c] += g_other[k]

    paused = {}

    def give_on(step):
        for r in order:
            number = 4 * step + r
            if number in BACK_STOPS:

                @pl.when(column == BACK_STOPS[number])
                def _():
                    arrive(PAUSE + number, pause.at[number])
                    paused[number].start()

    def give_back(step, r, grad):
        copy = remote(BACK + 4 * step + r, grad, back.at[step, at[r]], after)
        pl.when(column != HALF - 1)(copy.start)
        cols = pl.ds(pl.multiple_of(q * piece, piece), piece)
        target = member(there + SHIFTS - 2 - step, r)
        number = 4 * step + r
        if number in BACK_STOPS:
            leap = remote(
                BACK + number, grad, pause.at[number], (here + BACK_STOPS[number], t), PAUSE + number
            )
            onward = remote(
                PAUSE + number, pause.at[number], landed.at[:, cols], target, LAND + opposite(r)
            )
            paused[number] = onward
            inside.append((column == BACK_STOPS[number], onward))
        else:
            leap = remote(BACK + number, grad, landed.at[:, cols], target, LAND + opposite(r))
        pl.when(column == HALF - 1)(leap.start)
        started.append(copy)

    def returned(step, r):
        slot = back.at[step, at[r]]
        pl.when(column != 0)(remote(BACK + 4 * step + r, slot, slot, sib).wait_recv)
        slot[...] += g_image[2 - step, c, at[r]]

    @pl.when(column == 0)
    def _():
        back[...] = jnp.zeros_like(back)

    order = (2, 1, 3, 0)
    image_gradient((3,))
    sh_t, sl_t = sh.T, sl.T
    text_gradient(2)
    send(B_FAR_P, g_text.at[0, at[2]], far_in.at[0], up)
    send(B_FAR_M, g_text.at[1, at[2]], far_in.at[1], down)
    add_sibling(3)
    for r in order:
        give_back(0, r, g_image.at[3, c, at[r]])
    text_gradient(1)
    send(B_NEAR_P, g_text.at[1, at[1]], near_in.at[0], up)
    text_gradient(3)
    send(B_NEAR_M, g_text.at[0, at[3]], near_in.at[1], down)
    image_gradient((2,))
    image_gradient((0, 1))
    add_sibling(2)
    text_gradient(0)
    for r in order:
        returned(0, r)
        give_back(1, r, back.at[0, at[r]])
    add_sibling(1)
    add_sibling(0)
    arrive(B_FAR_P, far_in.at[0])
    g_text[0, at[1]] += far_in[0]
    send(B_SUM_P, g_text.at[0, at[1]], near_in.at[2], up)
    arrive(B_FAR_M, far_in.at[1])
    g_text[1, at[3]] += far_in[1]
    send(B_SUM_M, g_text.at[1, at[3]], near_in.at[3], down)
    for r in order:
        returned(1, r)
        give_back(2, r, back.at[1, at[r]])
    give_on(0)

    arrive(B_NEAR_P, near_in.at[0])
    arrive(B_NEAR_M, near_in.at[1])
    arrive(B_SUM_P, near_in.at[2])
    arrive(B_SUM_M, near_in.at[3])
    g_text[0, q] += near_in[1] + near_in[2]
    g_text[1, q] += near_in[0] + near_in[3]
    keep[...] = g_text[o, q]
    send(B_SIB, keep, half_of(gt_ref, c), sib)
    half_of(gt_ref, c)[...] = g_text[c, q]
    give_on(1)

    def own_columns(r, first=0, count=None):
        return piece_of(gi_ref, r, first, count)

    returned(2, 2)
    send(E_HALF_P, back.at[2, at[2], pl.ds(0, h)], half_in.at[2], up)
    send(E_HALF_M, back.at[2, at[2], pl.ds(h, h)], half_in.at[3], down)
    returned(2, 1)
    send(E_DIRECT_P, back.at[2, at[1]], own_columns(0), up)
    returned(2, 3)
    send(E_DIRECT_M, back.at[2, at[3]], own_columns(0), down)
    arrive(E_HALF_P, half_in.at[2])
    send(E_ON_P, half_in.at[2], own_columns(3, 0, h), up)
    arrive(E_HALF_M, half_in.at[3])
    send(E_ON_M, half_in.at[3], own_columns(1, h, h), down)
    returned(2, 0)
    own_columns(0)[...] = back[2, q]
    give_on(2)
    arrive(E_DIRECT_P, own_columns(3))
    arrive(E_DIRECT_M, own_columns(1))
    arrive(E_ON_P, own_columns(2, 0, h))
    arrive(E_ON_M, own_columns(2, h, h))
    arrive(B_SIB, half_of(gt_ref, o))

    @pl.when(column < SHIFTS - 1)
    def _():
        for r in range(N_Q):
            arrive(LAND + r, piece_of(landed, r))
        gi_ref[...] += landed[...]

    for copy in started:
        copy.wait_send()
    for guard, copy in inside:
        pl.when(guard)(copy.wait_send)


def shards(image_shard, text_shard, heat, bias):
    d, rows = image_shard.shape
    half, piece = rows // 2, rows // N_Q
    vmem = pl.BlockSpec(memory_space=pltpu.VMEM)
    smem = pl.BlockSpec(memory_space=pltpu.SMEM)
    hbm = pl.BlockSpec(memory_space=pl.ANY)
    n_dp = lax.axis_size("dp")

    def body(*refs):
        kernel(n_dp, *refs)

    return pl.pallas_call(
        body,
        out_shape=(jax.ShapeDtypeStruct((d, rows), F32), jax.ShapeDtypeStruct((d, rows), F32)),
        in_specs=[smem, smem, hbm, hbm],
        out_specs=(vmem, vmem),
        scratch_shapes=[
            pltpu.VMEM((2, N_Q, d, half), F32),
            pltpu.VMEM((SHIFTS, 2, N_Q, d, piece), F32),
            pltpu.VMEM((2, N_Q, d, half), BF16),
            pltpu.VMEM((2, N_Q, d, half), BF16),
            pltpu.VMEM((2, N_Q, d, rows), BF16),
            pltpu.VMEM((2, N_Q, d, rows), BF16),
            pltpu.VMEM((2, N_Q, d, half), F32),
            pltpu.VMEM((SHIFTS, 2, N_Q, d, piece), F32),
            pltpu.VMEM((SHIFTS, N_Q, d, piece), F32),
            pltpu.VMEM((SHIFTS - 1, N_Q, d, piece), F32),
            pltpu.VMEM((2, d, half), F32),
            pltpu.VMEM((4, d, half), F32),
            pltpu.VMEM((d, half), F32),
            pltpu.VMEM((4, d // 2, piece), F32),
            pltpu.VMEM((half, rows), F32),
            pltpu.VMEM((4 * (SHIFTS - 1), d, piece), F32),
            pltpu.VMEM((d, rows), F32),
            pltpu.VMEM((4 * (SHIFTS - 1), d, piece), F32),
            pltpu.SemaphoreType.DMA((N_SEMS,)),
            pltpu.SemaphoreType.DMA((N_SEMS,)),
            pltpu.SemaphoreType.DMA((2,)),
        ],
        compiler_params=pltpu.CompilerParams(
            collective_id=0, has_side_effects=True, vmem_limit_bytes=48 * 2**20
        ),
        name="window_gradients",
    )(heat, bias, image_shard, text_shard)


def solution(mesh):
    return jax.shard_map(
        shards,
        mesh=mesh,
        in_specs=(P("tensor", "dp"), P("tensor", "dp"), P(), P()),
        out_specs=(P("tensor", "dp"), P("tensor", "dp")),
        check_vma=False,
    )
```

```python
import jax
import jax.numpy as jnp
from jax import lax
from jax.experimental import pallas as pl
from jax.experimental.pallas import tpu as pltpu
from jax.sharding import PartitionSpec as P

SHIFTS = 4
N_Q = 4
MESH = pl.DeviceIdType.MESH
F32 = jnp.float32
BF16 = jnp.bfloat16

A_DIRECT_P, A_DIRECT_M, A_HALF_P, A_HALF_M, A_ON_P, A_ON_M = range(6)
T_SIB, T_OWN_P, T_OWN_M, T_SIB_P, T_SIB_M, T_ON_P, T_ON_M = range(6, 13)
B_FAR_P, B_FAR_M, B_NEAR_P, B_NEAR_M, B_SUM_P, B_SUM_M, B_SIB = range(13, 20)
E_DIRECT_P, E_DIRECT_M, E_HALF_P, E_HALF_M, E_ON_P, E_ON_M = range(20, 26)
G_SIB = 26
I_SIB = 30
CHAIN = 46
BACK = 58
STOP = 70
LAND = 82
PAUSE = 86
G_PART = 98
N_SEMS = 102

HALF = 32
BACK_STOPS = {1: 7, 3: 23, 0: 23, 5: 7, 7: 23, 4: 7, 9: 7, 8: 23}
STOPS = {0: 24, 3: 16, 1: 8, 2: 24, 4: 24, 7: 8, 8: 16, 11: 8}


def split(value):
    high = value.astype(BF16)
    return high, (value - high.astype(F32)).astype(BF16)


def dot3(a_high, a_low, b_high, b_low, dims):
    def one(a, b):
        return lax.dot_general(a, b, (dims, ((), ())), preferred_element_type=F32)

    return one(a_high, b_high) + (one(a_high, b_low) + one(a_low, b_high))


def kernel(
    n_dp,
    heat_ref,
    bias_ref,
    img_ref,
    txt_ref,
    gi_ref,
    gt_ref,
    text,
    image,
    t_high,
    t_low,
    i_high,
    i_low,
    g_text,
    g_image,
    g_other,
    back,
    far_in,
    near_in,
    keep,
    half_in,
    dots,
    stop,
    landed,
    pause,
    send_sem,
    recv_sem,
    local_sem,
):
    d, rows = img_ref.shape
    half, piece = rows // 2, rows // N_Q
    dp, t = lax.axis_index("dp"), lax.axis_index("tensor")
    q, c = t // 2, t % 2
    o = 1 - c
    at = [lax.rem(q + r, N_Q) for r in range(N_Q)]
    sib = (dp, 2 * q + o)
    up, down = (dp, 2 * at[1] + c), (dp, 2 * at[3] + c)
    after, before = (lax.rem(dp + 1, n_dp), t), (lax.rem(dp + n_dp - 1, n_dp), t)
    column = lax.rem(dp, HALF)
    here = dp - column
    there = HALF - here
    started = []

    def remote(index, src, dst, device, landing=None):
        return pltpu.make_async_remote_copy(
            src_ref=src,
            dst_ref=dst,
            send_sem=send_sem.at[index],
            recv_sem=recv_sem.at[index if landing is None else landing],
            device_id=device,
            device_id_type=MESH,
        )

    def send(index, src, dst, device):
        copy = remote(index, src, dst, device)
        copy.start()
        started.append(copy)

    def arrive(index, dst):
        remote(index, dst, dst, sib).wait_recv()

    def member(block, r):
        return (block, 2 * at[r] + c)

    def piece_of(ref, r, first=0, count=None):
        cols = pl.ds(pl.multiple_of(at[r] * piece, piece), piece)
        return ref.at[pl.ds(first, d if count is None else count), cols]

    def half_of(ref, which):
        return ref.at[:, pl.ds(pl.multiple_of(which * half, half), half)]

    own_piece = pltpu.make_async_copy(piece_of(img_ref, 0), image.at[0, c, q], local_sem.at[0])
    own_text = pltpu.make_async_copy(half_of(txt_ref, c), text.at[c, q], local_sem.at[1])
    own_piece.start()
    own_text.start()
    barrier = pltpu.get_barrier_semaphore()
    partners = (sib, up, down, after, before)
    for partner in partners:
        pl.semaphore_signal(barrier, inc=1, device_id=partner, device_id_type=MESH)
    greeted = len(partners)
    edge = HALF - 1
    meetings = [(k, there + edge, N_Q) for k in range(SHIFTS - 1)]
    meetings += [(edge, there + k, N_Q) for k in range(SHIFTS - 1)]
    for stop_at in sorted(set(STOPS.values())):
        meetings += [(0, here + stop_at, 1), (stop_at, here, 1)]
        meetings += [(edge, there + stop_at, 1), (stop_at, there + edge, 1)]
    for stop_at in sorted(set(BACK_STOPS.values())):
        meetings += [(edge, here + stop_at, 1), (stop_at, here + edge, 1)]
        for k in range(SHIFTS - 1):
            meetings += [(stop_at, there + k, N_Q), (k, there + stop_at, N_Q)]
    for where, block, count in meetings:

        @pl.when(column == where)
        def _():
            for r in range(count):
                pl.semaphore_signal(
                    barrier, inc=1, device_id=member(block, r), device_id_type=MESH
                )

        greeted += jnp.where(column == where, count, 0)
    pl.semaphore_wait(barrier, greeted)

    h = d // 2
    send(A_HALF_P, piece_of(img_ref, 2, 0, h), half_in.at[0], up)
    send(A_HALF_M, piece_of(img_ref, 2, h, h), half_in.at[1], down)

    inside = []

    def opposite(r):
        return (N_Q - r) % N_Q

    def chain(k, r):
        if k < SHIFTS - 1:
            number = 4 * k + r
            src, dst = image.at[k, c, at[r]], image.at[k + 1, c, at[r]]
            copy = remote(CHAIN + number, src, dst, before)
            started.append(copy)
            if number in STOPS:
                detour = remote(
                    CHAIN + number, src, stop.at[number], (here + STOPS[number], t), STOP + number
                )
                pl.when(column != 0)(copy.start)
                pl.when(column == 0)(detour.start)
            else:
                copy.start()
        send(I_SIB + 4 * k + r, image.at[k, c, at[r]], image.at[k, c, at[r]], sib)

    def chained(k, r):
        arrive(CHAIN + 4 * (k - 1) + r, image.at[k, c, at[r]])
        chain(k, r)

    def pass_edge(k, r):
        number = 4 * (k - 1) + r
        if number in STOPS:
            dst = image.at[k, c, at[r]]
            copy = remote(STOP + number, stop.at[number], dst, (there + edge, t), CHAIN + number)

            @pl.when(column == STOPS[number])
            def _():
                arrive(STOP + number, stop.at[number])
                copy.start()

            inside.append((column == STOPS[number], copy))

    own_piece.wait()
    chain(0, 0)
    send(A_DIRECT_P, piece_of(img_ref, 1), image.at[0, c, q], up)
    send(A_DIRECT_M, piece_of(img_ref, 3), image.at[0, c, q], down)
    send(T_SIB, half_of(txt_ref, o), text.at[c, q], sib)

    arrive(A_HALF_P, half_in.at[0])
    send(A_ON_P, half_in.at[0], image.at[0, c, at[3], pl.ds(0, h)], up)
    arrive(A_HALF_M, half_in.at[1])
    send(A_ON_M, half_in.at[1], image.at[0, c, at[1], pl.ds(h, h)], down)
    own_text.wait()
    send(T_OWN_P, text.at[c, q], text.at[c, q], up)
    arrive(T_SIB, text.at[o, q])
    send(T_SIB_M, text.at[o, q], text.at[o, q], down)

    pass_edge(1, 0)
    chained(1, 0)
    arrive(A_DIRECT_P, image.at[0, c, at[3]])
    chain(0, 3)
    arrive(A_DIRECT_M, image.at[0, c, at[1]])
    chain(0, 1)
    send(T_SIB_P, text.at[o, q], text.at[o, q], up)
    send(T_OWN_M, text.at[c, q], text.at[c, q], down)
    arrive(A_ON_P, image.at[0, c, at[2], pl.ds(0, h)])
    arrive(A_ON_M, image.at[0, c, at[2], pl.ds(h, h)])
    chain(0, 2)
    pass_edge(2, 0)
    chained(2, 0)
    pass_edge(1, 3)
    chained(1, 3)
    pass_edge(1, 1)
    chained(1, 1)
    arrive(T_OWN_P, text.at[c, at[3]])
    send(T_ON_P, text.at[c, at[3]], text.at[c, at[3]], up)
    arrive(T_SIB_M, text.at[o, at[1]])
    send(T_ON_M, text.at[o, at[1]], text.at[o, at[1]], down)
    pass_edge(1, 2)
    chained(1, 2)
    pass_edge(3, 0)
    chained(3, 0)
    pass_edge(2, 3)
    chained(2, 3)
    pass_edge(2, 1)
    chained(2, 1)
    pass_edge(2, 2)
    chained(2, 2)
    for r in (3, 1, 2):
        pass_edge(3, r)

    def text_ready(part, r):
        t_high[part, at[r]], t_low[part, at[r]] = split(text[part, at[r]])

    def image_ready(k, part, r):
        cols = slice(k * piece, (k + 1) * piece)
        i_high[part, at[r], :, cols], i_low[part, at[r], :, cols] = split(image[k, part, at[r]])

    def image_sibling(k, r):
        arrive(I_SIB + 4 * k + r, image.at[k, o, at[r]])
        image_ready(k, o, r)

    text_ready(c, 0)
    text_ready(o, 0)
    text_ready(c, 3)
    text_ready(o, 1)
    for k in range(SHIFTS - 1):
        for r in (0, 3, 1, 2):
            image_ready(k, c, r)
            image_sibling(k, r)
    for r in (3, 1, 2):
        chained(3, r)
    for r in (0, 3, 1, 2):
        image_ready(3, c, r)
        image_sibling(3, r)
    arrive(T_SIB_P, text.at[o, at[3]])
    text_ready(o, 3)
    arrive(T_OWN_M, text.at[c, at[1]])
    text_ready(c, 1)

    def quarter_dots(r):
        def rows_of(ref):
            return ref[:, at[r]].reshape(2 * d, ref.shape[-1])

        return dot3(
            rows_of(t_high), rows_of(t_low), rows_of(i_high), rows_of(i_low), ((0,), (0,))
        )

    dots[...] = quarter_dots(0) + quarter_dots(3) + quarter_dots(1)
    arrive(T_ON_P, text.at[c, at[2]])
    text_ready(c, 2)
    arrive(T_ON_M, text.at[o, at[2]])
    text_ready(o, 2)

    depth = 2 * N_Q * d
    th, tl = t_high[...].reshape(depth, half), t_low[...].reshape(depth, half)
    heat = jnp.exp(jnp.full((1, rows), heat_ref[0], F32))
    slope = jax.nn.sigmoid(heat * (dots[...] + quarter_dots(2)) + bias_ref[0])
    text_id = lax.broadcasted_iota(jnp.int32, slope.shape, 0) + c * half
    image_id = lax.broadcasted_iota(jnp.int32, slope.shape, 1)
    match = (image_id < piece) & (text_id == image_id + q * piece)
    slope = heat * (slope - jnp.where(match, 1.0, 0.0).astype(F32))
    sh, sl = split(slope)

    order = (2, 1, 3, 0)

    def image_gradient(ks):
        lo, hi = ks[0] * piece, (ks[-1] + 1) * piece
        grad = dot3(th, tl, sh[:, lo:hi], sl[:, lo:hi], ((1,), (0,)))
        grad = grad.reshape(2, N_Q, d, hi - lo)
        for i, k in enumerate(ks):
            g_image[k] = grad[..., i * piece : (i + 1) * piece]
            if k < 3:
                send(G_SIB + k, g_image.at[k, o], g_other.at[k], sib)
                continue
            for r in order:
                send(G_PART + r, g_image.at[k, o, at[r]], g_other.at[k, at[r]], sib)

    def text_gradient(r):
        high, low = (ref[:, at[r]].reshape(2 * d, rows) for ref in (i_high, i_low))
        g_text[:, at[r]] = dot3(high, low, sh_t, sl_t, ((1,), (0,))).reshape(2, d, half)

    def add_sibling(k):
        arrive(G_SIB + k, g_other.at[k])
        g_image[k, c] += g_other[k]

    paused = {}

    def give_on(step):
        for r in order:
            number = 4 * step + r
            if number in BACK_STOPS:

                @pl.when(column == BACK_STOPS[number])
                def _():
                    arrive(PAUSE + number, pause.at[number])
                    paused[number].start()

    def give_back(step, r, grad):
        copy = remote(BACK + 4 * step + r, grad, back.at[step, at[r]], after)
        pl.when(column != HALF - 1)(copy.start)
        cols = pl.ds(pl.multiple_of(q * piece, piece), piece)
        target = member(there + SHIFTS - 2 - step, r)
        number = 4 * step + r
        if number in BACK_STOPS:
            leap = remote(
                BACK + number, grad, pause.at[number], (here + BACK_STOPS[number], t), PAUSE + number
            )
            onward = remote(
                PAUSE + number, pause.at[number], landed.at[:, cols], target, LAND + opposite(r)
            )
            paused[number] = onward
            inside.append((column == BACK_STOPS[number], onward))
        else:
            leap = remote(BACK + number, grad, landed.at[:, cols], target, LAND + opposite(r))
        pl.when(column == HALF - 1)(leap.start)
        started.append(copy)

    def returned(step, r):
        slot = back.at[step, at[r]]
        pl.when(column != 0)(remote(BACK + 4 * step + r, slot, slot, sib).wait_recv)
        slot[...] += g_image[2 - step, c, at[r]]

    @pl.when(column == 0)
    def _():
        back[...] = jnp.zeros_like(back)

    sh_t, sl_t = sh.T, sl.T
    text_gradient(2)
    send(B_FAR_P, g_text.at[0, at[2]], far_in.at[0], up)
    send(B_FAR_M, g_text.at[1, at[2]], far_in.at[1], down)
    image_gradient((3,))
    for r in order:
        arrive(G_PART + r, g_other.at[3, at[r]])
        g_image[3, c, at[r]] += g_other[3, at[r]]
        give_back(0, r, g_image.at[3, c, at[r]])
    text_gradient(1)
    send(B_NEAR_P, g_text.at[1, at[1]], near_in.at[0], up)
    text_gradient(3)
    send(B_NEAR_M, g_text.at[0, at[3]], near_in.at[1], down)
    image_gradient((2,))
    image_gradient((0, 1))
    add_sibling(2)
    text_gradient(0)
    for r in order:
        returned(0, r)
        give_back(1, r, back.at[0, at[r]])
    add_sibling(1)
    add_sibling(0)
    arrive(B_FAR_P, far_in.at[0])
    g_text[0, at[1]] += far_in[0]
    send(B_SUM_P, g_text.at[0, at[1]], near_in.at[2], up)
    arrive(B_FAR_M, far_in.at[1])
    g_text[1, at[3]] += far_in[1]
    send(B_SUM_M, g_text.at[1, at[3]], near_in.at[3], down)
    for r in order:
        returned(1, r)
        give_back(2, r, back.at[1, at[r]])
    give_on(0)

    arrive(B_NEAR_P, near_in.at[0])
    arrive(B_NEAR_M, near_in.at[1])
    arrive(B_SUM_P, near_in.at[2])
    arrive(B_SUM_M, near_in.at[3])
    g_text[0, q] += near_in[1] + near_in[2]
    g_text[1, q] += near_in[0] + near_in[3]
    keep[...] = g_text[o, q]
    send(B_SIB, keep, half_of(gt_ref, c), sib)
    half_of(gt_ref, c)[...] = g_text[c, q]
    give_on(1)

    def own_columns(r, first=0, count=None):
        return piece_of(gi_ref, r, first, count)

    returned(2, 2)
    send(E_HALF_P, back.at[2, at[2], pl.ds(0, h)], half_in.at[2], up)
    send(E_HALF_M, back.at[2, at[2], pl.ds(h, h)], half_in.at[3], down)
    returned(2, 1)
    send(E_DIRECT_P, back.at[2, at[1]], own_columns(0), up)
    returned(2, 3)
    send(E_DIRECT_M, back.at[2, at[3]], own_columns(0), down)
    arrive(E_HALF_P, half_in.at[2])
    send(E_ON_P, half_in.at[2], own_columns(3, 0, h), up)
    arrive(E_HALF_M, half_in.at[3])
    send(E_ON_M, half_in.at[3], own_columns(1, h, h), down)
    returned(2, 0)
    own_columns(0)[...] = back[2, q]
    give_on(2)
    arrive(E_DIRECT_P, own_columns(3))
    arrive(E_DIRECT_M, own_columns(1))
    arrive(E_ON_P, own_columns(2, 0, h))
    arrive(E_ON_M, own_columns(2, h, h))
    arrive(B_SIB, half_of(gt_ref, o))

    @pl.when(column < SHIFTS - 1)
    def _():
        for r in range(N_Q):
            arrive(LAND + r, piece_of(landed, r))
        gi_ref[...] += landed[...]

    for copy in started:
        copy.wait_send()
    for guard, copy in inside:
        pl.when(guard)(copy.wait_send)


def shards(image_shard, text_shard, heat, bias):
    d, rows = image_shard.shape
    half, piece = rows // 2, rows // N_Q
    vmem = pl.BlockSpec(memory_space=pltpu.VMEM)
    smem = pl.BlockSpec(memory_space=pltpu.SMEM)
    hbm = pl.BlockSpec(memory_space=pl.ANY)
    n_dp = lax.axis_size("dp")

    def body(*refs):
        kernel(n_dp, *refs)

    return pl.pallas_call(
        body,
        out_shape=(jax.ShapeDtypeStruct((d, rows), F32), jax.ShapeDtypeStruct((d, rows), F32)),
        in_specs=[smem, smem, hbm, hbm],
        out_specs=(vmem, vmem),
        scratch_shapes=[
            pltpu.VMEM((2, N_Q, d, half), F32),
            pltpu.VMEM((SHIFTS, 2, N_Q, d, piece), F32),
            pltpu.VMEM((2, N_Q, d, half), BF16),
            pltpu.VMEM((2, N_Q, d, half), BF16),
            pltpu.VMEM((2, N_Q, d, rows), BF16),
            pltpu.VMEM((2, N_Q, d, rows), BF16),
            pltpu.VMEM((2, N_Q, d, half), F32),
            pltpu.VMEM((SHIFTS, 2, N_Q, d, piece), F32),
            pltpu.VMEM((SHIFTS, N_Q, d, piece), F32),
            pltpu.VMEM((SHIFTS - 1, N_Q, d, piece), F32),
            pltpu.VMEM((2, d, half), F32),
            pltpu.VMEM((4, d, half), F32),
            pltpu.VMEM((d, half), F32),
            pltpu.VMEM((4, d // 2, piece), F32),
            pltpu.VMEM((half, rows), F32),
            pltpu.VMEM((4 * (SHIFTS - 1), d, piece), F32),
            pltpu.VMEM((d, rows), F32),
            pltpu.VMEM((4 * (SHIFTS - 1), d, piece), F32),
            pltpu.SemaphoreType.DMA((N_SEMS,)),
            pltpu.SemaphoreType.DMA((N_SEMS,)),
            pltpu.SemaphoreType.DMA((2,)),
        ],
        compiler_params=pltpu.CompilerParams(
            collective_id=0, has_side_effects=True, vmem_limit_bytes=48 * 2**20
        ),
        name="window_gradients",
    )(heat, bias, image_shard, text_shard)


def solution(mesh):
    return jax.shard_map(
        shards,
        mesh=mesh,
        in_specs=(P("tensor", "dp"), P("tensor", "dp"), P(), P()),
        out_specs=(P("tensor", "dp"), P("tensor", "dp")),
        check_vma=False,
    )
```

```python
import jax
import jax.numpy as jnp
from jax import lax
from jax.experimental import pallas as pl
from jax.experimental.pallas import tpu as pltpu
from jax.sharding import PartitionSpec as P

SHIFTS = 4
N_Q = 4
MESH = pl.DeviceIdType.MESH
F32 = jnp.float32
BF16 = jnp.bfloat16

A_DIRECT_P, A_DIRECT_M, A_HALF_P, A_HALF_M, A_ON_P, A_ON_M = range(6)
T_SIB, T_OWN_P, T_OWN_M, T_SIB_P, T_SIB_M, T_ON_P, T_ON_M = range(6, 13)
B_FAR_P, B_FAR_M, B_NEAR_P, B_NEAR_M, B_SUM_P, B_SUM_M, B_SIB = range(13, 20)
E_DIRECT_P, E_DIRECT_M, E_HALF_P, E_HALF_M, E_ON_P, E_ON_M = range(20, 26)
G_SIB = 26
I_SIB = 30
CHAIN = 46
BACK = 58
STOP = 70
LAND = 82
PAUSE = 86
G_PART = 98
N_SEMS = 102

HALF = 32
BACK_STOPS = {1: 7, 3: 23, 0: 23, 5: 7, 7: 23, 4: 7, 9: 7, 8: 23}
STOPS = {0: 24, 3: 16, 1: 8, 2: 24, 4: 24, 7: 8, 8: 24, 11: 8}


def split(value):
    high = value.astype(BF16)
    return high, (value - high.astype(F32)).astype(BF16)


def dot3(a_high, a_low, b_high, b_low, dims):
    def one(a, b):
        return lax.dot_general(a, b, (dims, ((), ())), preferred_element_type=F32)

    return one(a_high, b_high) + (one(a_high, b_low) + one(a_low, b_high))


def kernel(
    n_dp,
    heat_ref,
    bias_ref,
    img_ref,
    txt_ref,
    gi_ref,
    gt_ref,
    text,
    image,
    t_high,
    t_low,
    i_high,
    i_low,
    g_text,
    g_image,
    g_other,
    back,
    far_in,
    near_in,
    keep,
    half_in,
    dots,
    stop,
    landed,
    pause,
    send_sem,
    recv_sem,
    local_sem,
):
    d, rows = img_ref.shape
    half, piece = rows // 2, rows // N_Q
    dp, t = lax.axis_index("dp"), lax.axis_index("tensor")
    q, c = t // 2, t % 2
    o = 1 - c
    at = [lax.rem(q + r, N_Q) for r in range(N_Q)]
    sib = (dp, 2 * q + o)
    up, down = (dp, 2 * at[1] + c), (dp, 2 * at[3] + c)
    after, before = (lax.rem(dp + 1, n_dp), t), (lax.rem(dp + n_dp - 1, n_dp), t)
    column = lax.rem(dp, HALF)
    here = dp - column
    there = HALF - here
    started = []

    def remote(index, src, dst, device, landing=None):
        return pltpu.make_async_remote_copy(
            src_ref=src,
            dst_ref=dst,
            send_sem=send_sem.at[index],
            recv_sem=recv_sem.at[index if landing is None else landing],
            device_id=device,
            device_id_type=MESH,
        )

    def send(index, src, dst, device):
        copy = remote(index, src, dst, device)
        copy.start()
        started.append(copy)

    def arrive(index, dst):
        remote(index, dst, dst, sib).wait_recv()

    def member(block, r):
        return (block, 2 * at[r] + c)

    def piece_of(ref, r, first=0, count=None):
        cols = pl.ds(pl.multiple_of(at[r] * piece, piece), piece)
        return ref.at[pl.ds(first, d if count is None else count), cols]

    def half_of(ref, which):
        return ref.at[:, pl.ds(pl.multiple_of(which * half, half), half)]

    own_piece = pltpu.make_async_copy(piece_of(img_ref, 0), image.at[0, c, q], local_sem.at[0])
    own_text = pltpu.make_async_copy(half_of(txt_ref, c), text.at[c, q], local_sem.at[1])
    own_piece.start()
    own_text.start()
    barrier = pltpu.get_barrier_semaphore()
    partners = (sib, up, down, after, before)
    for partner in partners:
        pl.semaphore_signal(barrier, inc=1, device_id=partner, device_id_type=MESH)
    greeted = len(partners)
    edge = HALF - 1
    meetings = [(k, there + edge, N_Q) for k in range(SHIFTS - 1)]
    meetings += [(edge, there + k, N_Q) for k in range(SHIFTS - 1)]
    for stop_at in sorted(set(STOPS.values())):
        meetings += [(0, here + stop_at, 1), (stop_at, here, 1)]
        meetings += [(edge, there + stop_at, 1), (stop_at, there + edge, 1)]
    for stop_at in sorted(set(BACK_STOPS.values())):
        meetings += [(edge, here + stop_at, 1), (stop_at, here + edge, 1)]
        for k in range(SHIFTS - 1):
            meetings += [(stop_at, there + k, N_Q), (k, there + stop_at, N_Q)]
    for where, block, count in meetings:

        @pl.when(column == where)
        def _():
            for r in range(count):
                pl.semaphore_signal(
                    barrier, inc=1, device_id=member(block, r), device_id_type=MESH
                )

        greeted += jnp.where(column == where, count, 0)
    pl.semaphore_wait(barrier, greeted)

    h = d // 2
    send(A_HALF_P, piece_of(img_ref, 2, 0, h), half_in.at[0], up)
    send(A_HALF_M, piece_of(img_ref, 2, h, h), half_in.at[1], down)

    inside = []

    def opposite(r):
        return (N_Q - r) % N_Q

    def chain(k, r):
        if k < SHIFTS - 1:
            number = 4 * k + r
            src, dst = image.at[k, c, at[r]], image.at[k + 1, c, at[r]]
            copy = remote(CHAIN + number, src, dst, before)
            started.append(copy)
            if number in STOPS:
                detour = remote(
                    CHAIN + number, src, stop.at[number], (here + STOPS[number], t), STOP + number
                )
                pl.when(column != 0)(copy.start)
                pl.when(column == 0)(detour.start)
            else:
                copy.start()
        send(I_SIB + 4 * k + r, image.at[k, c, at[r]], image.at[k, c, at[r]], sib)

    def chained(k, r):
        arrive(CHAIN + 4 * (k - 1) + r, image.at[k, c, at[r]])
        chain(k, r)

    def pass_edge(k, r):
        number = 4 * (k - 1) + r
        if number in STOPS:
            dst = image.at[k, c, at[r]]
            copy = remote(STOP + number, stop.at[number], dst, (there + edge, t), CHAIN + number)

            @pl.when(column == STOPS[number])
            def _():
                arrive(STOP + number, stop.at[number])
                copy.start()

            inside.append((column == STOPS[number], copy))

    own_piece.wait()
    chain(0, 0)
    send(A_DIRECT_P, piece_of(img_ref, 1), image.at[0, c, q], up)
    send(A_DIRECT_M, piece_of(img_ref, 3), image.at[0, c, q], down)
    send(T_SIB, half_of(txt_ref, o), text.at[c, q], sib)

    arrive(A_HALF_P, half_in.at[0])
    send(A_ON_P, half_in.at[0], image.at[0, c, at[3], pl.ds(0, h)], up)
    arrive(A_HALF_M, half_in.at[1])
    send(A_ON_M, half_in.at[1], image.at[0, c, at[1], pl.ds(h, h)], down)
    own_text.wait()
    send(T_OWN_P, text.at[c, q], text.at[c, q], up)
    arrive(T_SIB, text.at[o, q])
    send(T_SIB_M, text.at[o, q], text.at[o, q], down)

    pass_edge(1, 0)
    chained(1, 0)
    arrive(A_DIRECT_P, image.at[0, c, at[3]])
    chain(0, 3)
    arrive(A_DIRECT_M, image.at[0, c, at[1]])
    chain(0, 1)
    send(T_SIB_P, text.at[o, q], text.at[o, q], up)
    send(T_OWN_M, text.at[c, q], text.at[c, q], down)
    arrive(A_ON_P, image.at[0, c, at[2], pl.ds(0, h)])
    arrive(A_ON_M, image.at[0, c, at[2], pl.ds(h, h)])
    chain(0, 2)
    pass_edge(2, 0)
    chained(2, 0)
    pass_edge(1, 3)
    chained(1, 3)
    pass_edge(1, 1)
    chained(1, 1)
    arrive(T_OWN_P, text.at[c, at[3]])
    send(T_ON_P, text.at[c, at[3]], text.at[c, at[3]], up)
    arrive(T_SIB_M, text.at[o, at[1]])
    send(T_ON_M, text.at[o, at[1]], text.at[o, at[1]], down)
    pass_edge(1, 2)
    chained(1, 2)
    pass_edge(3, 0)
    chained(3, 0)
    pass_edge(2, 3)
    chained(2, 3)
    pass_edge(2, 1)
    chained(2, 1)
    pass_edge(2, 2)
    chained(2, 2)
    for r in (3, 1, 2):
        pass_edge(3, r)

    def text_ready(part, r):
        t_high[part, at[r]], t_low[part, at[r]] = split(text[part, at[r]])

    def image_ready(k, part, r):
        cols = slice(k * piece, (k + 1) * piece)
        i_high[part, at[r], :, cols], i_low[part, at[r], :, cols] = split(image[k, part, at[r]])

    def image_sibling(k, r):
        arrive(I_SIB + 4 * k + r, image.at[k, o, at[r]])
        image_ready(k, o, r)

    text_ready(c, 0)
    text_ready(o, 0)
    text_ready(c, 3)
    text_ready(o, 1)
    for k in range(SHIFTS - 1):
        for r in (0, 3, 1, 2):
            image_ready(k, c, r)
            image_sibling(k, r)
    for r in (3, 1, 2):
        chained(3, r)
    for r in (0, 3, 1, 2):
        image_ready(3, c, r)
        image_sibling(3, r)
    arrive(T_SIB_P, text.at[o, at[3]])
    text_ready(o, 3)
    arrive(T_OWN_M, text.at[c, at[1]])
    text_ready(c, 1)

    def quarter_dots(r):
        def rows_of(ref):
            return ref[:, at[r]].reshape(2 * d, ref.shape[-1])

        return dot3(
            rows_of(t_high), rows_of(t_low), rows_of(i_high), rows_of(i_low), ((0,), (0,))
        )

    dots[...] = quarter_dots(0) + quarter_dots(3) + quarter_dots(1)
    arrive(T_ON_P, text.at[c, at[2]])
    text_ready(c, 2)
    arrive(T_ON_M, text.at[o, at[2]])
    text_ready(o, 2)

    depth = 2 * N_Q * d
    th, tl = t_high[...].reshape(depth, half), t_low[...].reshape(depth, half)
    heat = jnp.exp(jnp.full((1, rows), heat_ref[0], F32))
    slope = jax.nn.sigmoid(heat * (dots[...] + quarter_dots(2)) + bias_ref[0])
    text_id = lax.broadcasted_iota(jnp.int32, slope.shape, 0) + c * half
    image_id = lax.broadcasted_iota(jnp.int32, slope.shape, 1)
    match = (image_id < piece) & (text_id == image_id + q * piece)
    slope = heat * (slope - jnp.where(match, 1.0, 0.0).astype(F32))
    sh, sl = split(slope)

    order = (2, 1, 3, 0)

    def image_gradient(ks):
        lo, hi = ks[0] * piece, (ks[-1] + 1) * piece
        grad = dot3(th, tl, sh[:, lo:hi], sl[:, lo:hi], ((1,), (0,)))
        grad = grad.reshape(2, N_Q, d, hi - lo)
        for i, k in enumerate(ks):
            g_image[k] = grad[..., i * piece : (i + 1) * piece]
            if k < 3:
                send(G_SIB + k, g_image.at[k, o], g_other.at[k], sib)
                continue
            for r in order:
                send(G_PART + r, g_image.at[k, o, at[r]], g_other.at[k, at[r]], sib)

    def text_gradient(r):
        high, low = (ref[:, at[r]].reshape(2 * d, rows) for ref in (i_high, i_low))
        g_text[:, at[r]] = dot3(high, low, sh_t, sl_t, ((1,), (0,))).reshape(2, d, half)

    def add_sibling(k):
        arrive(G_SIB + k, g_other.at[k])
        g_image[k, c] += g_other[k]

    paused = {}

    def give_on(step):
        for r in order:
            number = 4 * step + r
            if number in BACK_STOPS:

                @pl.when(column == BACK_STOPS[number])
                def _():
                    arrive(PAUSE + number, pause.at[number])
                    paused[number].start()

    def give_back(step, r, grad):
        copy = remote(BACK + 4 * step + r, grad, back.at[step, at[r]], after)
        pl.when(column != HALF - 1)(copy.start)
        cols = pl.ds(pl.multiple_of(q * piece, piece), piece)
        target = member(there + SHIFTS - 2 - step, r)
        number = 4 * step + r
        if number in BACK_STOPS:
            leap = remote(
                BACK + number, grad, pause.at[number], (here + BACK_STOPS[number], t), PAUSE + number
            )
            onward = remote(
                PAUSE + number, pause.at[number], landed.at[:, cols], target, LAND + opposite(r)
            )
            paused[number] = onward
            inside.append((column == BACK_STOPS[number], onward))
        else:
            leap = remote(BACK + number, grad, landed.at[:, cols], target, LAND + opposite(r))
        pl.when(column == HALF - 1)(leap.start)
        started.append(copy)

    def returned(step, r):
        slot = back.at[step, at[r]]
        pl.when(column != 0)(remote(BACK + 4 * step + r, slot, slot, sib).wait_recv)
        slot[...] += g_image[2 - step, c, at[r]]

    @pl.when(column == 0)
    def _():
        back[...] = jnp.zeros_like(back)

    sh_t, sl_t = sh.T, sl.T
    text_gradient(2)
    send(B_FAR_P, g_text.at[0, at[2]], far_in.at[0], up)
    send(B_FAR_M, g_text.at[1, at[2]], far_in.at[1], down)
    image_gradient((3,))
    for r in order:
        arrive(G_PART + r, g_other.at[3, at[r]])
        g_image[3, c, at[r]] += g_other[3, at[r]]
        give_back(0, r, g_image.at[3, c, at[r]])
    text_gradient(1)
    send(B_NEAR_P, g_text.at[1, at[1]], near_in.at[0], up)
    text_gradient(3)
    send(B_NEAR_M, g_text.at[0, at[3]], near_in.at[1], down)
    image_gradient((2,))
    image_gradient((0, 1))
    add_sibling(2)
    text_gradient(0)
    for r in order:
        returned(0, r)
        give_back(1, r, back.at[0, at[r]])
    add_sibling(1)
    add_sibling(0)
    arrive(B_FAR_P, far_in.at[0])
    g_text[0, at[1]] += far_in[0]
    send(B_SUM_P, g_text.at[0, at[1]], near_in.at[2], up)
    arrive(B_FAR_M, far_in.at[1])
    g_text[1, at[3]] += far_in[1]
    send(B_SUM_M, g_text.at[1, at[3]], near_in.at[3], down)
    for r in order:
        returned(1, r)
        give_back(2, r, back.at[1, at[r]])
    give_on(0)

    arrive(B_NEAR_P, near_in.at[0])
    arrive(B_NEAR_M, near_in.at[1])
    arrive(B_SUM_P, near_in.at[2])
    arrive(B_SUM_M, near_in.at[3])
    g_text[0, q] += near_in[1] + near_in[2]
    g_text[1, q] += near_in[0] + near_in[3]
    keep[...] = g_text[o, q]
    send(B_SIB, keep, half_of(gt_ref, c), sib)
    half_of(gt_ref, c)[...] = g_text[c, q]
    give_on(1)

    def own_columns(r, first=0, count=None):
        return piece_of(gi_ref, r, first, count)

    returned(2, 2)
    send(E_HALF_P, back.at[2, at[2], pl.ds(0, h)], half_in.at[2], up)
    send(E_HALF_M, back.at[2, at[2], pl.ds(h, h)], half_in.at[3], down)
    returned(2, 1)
    send(E_DIRECT_P, back.at[2, at[1]], own_columns(0), up)
    returned(2, 3)
    send(E_DIRECT_M, back.at[2, at[3]], own_columns(0), down)
    arrive(E_HALF_P, half_in.at[2])
    send(E_ON_P, half_in.at[2], own_columns(3, 0, h), up)
    arrive(E_HALF_M, half_in.at[3])
    send(E_ON_M, half_in.at[3], own_columns(1, h, h), down)
    returned(2, 0)
    own_columns(0)[...] = back[2, q]
    give_on(2)
    arrive(E_DIRECT_P, own_columns(3))
    arrive(E_DIRECT_M, own_columns(1))
    arrive(E_ON_P, own_columns(2, 0, h))
    arrive(E_ON_M, own_columns(2, h, h))
    arrive(B_SIB, half_of(gt_ref, o))

    @pl.when(column < SHIFTS - 1)
    def _():
        for r in range(N_Q):
            arrive(LAND + r, piece_of(landed, r))
        gi_ref[...] += landed[...]

    for copy in started:
        copy.wait_send()
    for guard, copy in inside:
        pl.when(guard)(copy.wait_send)


def shards(image_shard, text_shard, heat, bias):
    d, rows = image_shard.shape
    half, piece = rows // 2, rows // N_Q
    vmem = pl.BlockSpec(memory_space=pltpu.VMEM)
    smem = pl.BlockSpec(memory_space=pltpu.SMEM)
    hbm = pl.BlockSpec(memory_space=pl.ANY)
    n_dp = lax.axis_size("dp")

    def body(*refs):
        kernel(n_dp, *refs)

    return pl.pallas_call(
        body,
        out_shape=(jax.ShapeDtypeStruct((d, rows), F32), jax.ShapeDtypeStruct((d, rows), F32)),
        in_specs=[smem, smem, hbm, hbm],
        out_specs=(vmem, vmem),
        scratch_shapes=[
            pltpu.VMEM((2, N_Q, d, half), F32),
            pltpu.VMEM((SHIFTS, 2, N_Q, d, piece), F32),
            pltpu.VMEM((2, N_Q, d, half), BF16),
            pltpu.VMEM((2, N_Q, d, half), BF16),
            pltpu.VMEM((2, N_Q, d, rows), BF16),
            pltpu.VMEM((2, N_Q, d, rows), BF16),
            pltpu.VMEM((2, N_Q, d, half), F32),
            pltpu.VMEM((SHIFTS, 2, N_Q, d, piece), F32),
            pltpu.VMEM((SHIFTS, N_Q, d, piece), F32),
            pltpu.VMEM((SHIFTS - 1, N_Q, d, piece), F32),
            pltpu.VMEM((2, d, half), F32),
            pltpu.VMEM((4, d, half), F32),
            pltpu.VMEM((d, half), F32),
            pltpu.VMEM((4, d // 2, piece), F32),
            pltpu.VMEM((half, rows), F32),
            pltpu.VMEM((4 * (SHIFTS - 1), d, piece), F32),
            pltpu.VMEM((d, rows), F32),
            pltpu.VMEM((4 * (SHIFTS - 1), d, piece), F32),
            pltpu.SemaphoreType.DMA((N_SEMS,)),
            pltpu.SemaphoreType.DMA((N_SEMS,)),
            pltpu.SemaphoreType.DMA((2,)),
        ],
        compiler_params=pltpu.CompilerParams(
            collective_id=0, has_side_effects=True, vmem_limit_bytes=48 * 2**20
        ),
        name="window_gradients",
    )(heat, bias, image_shard, text_shard)


def solution(mesh):
    return jax.shard_map(
        shards,
        mesh=mesh,
        in_specs=(P("tensor", "dp"), P("tensor", "dp"), P(), P()),
        out_specs=(P("tensor", "dp"), P("tensor", "dp")),
        check_vma=False,
    )
```
